32 devices in a mesh: grp: 2 (over y), dev: 16 (over z, x, core).
Axes of the slice: x: 2, y: 2, z: 4, core: 2. Of those that a mesh axis runs over, the one named last changes fastest.
Arguments:
- leaf_right: float32 [32, 8192], P(None, ('grp', 'dev')), may hold values from -6 to 6
- leaf_inverse: float32 [64, 128, 128], P(('grp', 'dev')), may hold values from -1 to 2, as said below
- leaf_link: float32 [64, 128, 128], P(('grp', 'dev')), may hold values from -0.25 to 0.25
- leaf_front: float32 [64, 128, 128], P(('grp', 'dev')), may hold values from -0.375 to 0.375
- parents: int32 [64], P(('grp', 'dev')), may hold values from 1 to 2, as said below
- front_rows: int32 [64], P(('grp', 'dev')), may hold values from 0 to 15
- live_blocks: int32 [32], P(('grp', 'dev')), may hold values from 1 to 2, 56 in all
- front_right: float32 [32, 4096], P(None, ('grp', 'dev')), may hold values from -6 to 6
- front_inverse: float32 [4096, 2048], P(('grp', 'dev')), may hold values from -1 to 2, as said below
- front_couple: float32 [4096, 4096], P(('grp', 'dev')), may hold values from -0.09375 to 0.09375
- root_right: float32 [32, 2, 2048], P(None, None, 'dev'), may hold values from -6 to 6
- root_inverse: float32 [2, 2048, 2048], P(None, 'dev', 'grp'), may hold values from -1 to 2, as said below
- root_couple: float32 [1, 2048, 2048], P(None, 'dev', 'grp'), may hold values from -0.09375 to 0.09375
Outputs:
- leaf_solution: float32 [32, 8192], P(None, ('grp', 'dev'))
- front_solution: float32 [32, 4096], P(None, 'grp')
- root_solution: float32 [32, 2, 2048], P(None, None, 'dev')
The draws below stay inside these ranges and needn't reach their ends.
Inputs may be any that keep to these rules, and one draw needn't show every extreme that they name: For local block k = b mod 2, parents[b] lies in k + 1 .. 2; the value 2 means no parent among the piece's blocks. A piece's live blocks are its first live_blocks[p]; some piece has all 2. `leaf_inverse`: each block is lower triangular with a positive diagonal. `front_inverse`: each front's block is lower triangular with a positive diagonal. `root_inverse`: each level's block is lower triangular with a positive diagonal.
All inputs are finite; a program needn't handle non-finite values.
Results may differ from the reference program's by a relative error of at most 0.0003.
Values sent between devices are 32-bit elements; how exact they have to be, the bound alone decides.
A program may use at most 64 MiB of HBM per device.

```python
import math
import jax
import jax.numpy as jnp
import numpy as np
from jax import lax

NB = 128
RIGHT_SIDES = 32
SB = 2
FBG = 16
CHAIN_LEVELS = 2
FG = 2048
LEVEL_ROWS = 2048
DEVS = 32
NSUB = 64
GROWS = 4096
NPAIR = 1
FEEDS = 2
LIVE_TOTAL = 56
N_GRP = 2
N_DEV = 16


def lower_inverse(key, salt, blocks_count, order):
    first_key, second_key = jax.random.split(jax.random.fold_in(key, salt))
    scales = jnp.exp(jax.random.uniform(first_key, (blocks_count, order), jnp.float32, math.log(0.6), math.log(1.4)))
    noise = jax.random.normal(second_key, (blocks_count, order, order), jnp.float32)
    noise = jnp.clip(noise, -4.0, 4.0)
    lower = jnp.tril(noise * (0.5 / math.sqrt(order)), -1)
    return lower + jnp.eye(order, dtype=jnp.float32)[None] * scales[:, None, :]


def draw_leaf_inverse(key, part):
    return lower_inverse(key, 17, NSUB, NB)


def draw_front_inverse(key, part):
    return lower_inverse(key, 23, GROWS // FG, FG).reshape(GROWS, FG)


def draw_root_inverse(key, part):
    return lower_inverse(key, 31, CHAIN_LEVELS, LEVEL_ROWS)


def draw_parents(key, part):
    place = jnp.arange(NSUB, dtype=jnp.int32) % SB
    spans = SB - place
    offsets = jax.random.randint(jax.random.fold_in(key, 29), (NSUB,), 0, spans, dtype=jnp.int32)
    return (place + 1 + offsets).astype(jnp.int32)


def set_ends(values, rng, least, largest):
    spot = [jax.random.randint(jax.random.fold_in(rng, axis), (), 0, length) for axis, length in enumerate(values.shape)]
    longest = values.shape.index(max(values.shape))
    beside = spot[:longest] + [(spot[longest] + 1) % values.shape[longest]] + spot[longest + 1:]
    return values.at[tuple(spot)].set(least).at[tuple(beside)].set(largest)


def levels(key, dims, shards, smallest, top_value):
    def one(dim, parts):
        heights = jax.random.uniform(jax.random.fold_in(jax.random.fold_in(key, 6), dim), (parts,), jnp.float32, smallest / len(shards), top_value / len(shards))
        return jnp.repeat(jnp.exp(heights), dims[dim] // parts).reshape((-1,) + (1,) * (len(dims) - dim - 1))

    level = one(*shards[0])
    for cut in shards[1:]:
        level = level * one(*cut)
    return level


def length_profile(number_of, total, most, slope):
    portions = [(1 << 20) // math.isqrt(grade ** slope) + 1 for grade in range(2, number_of + 1)]
    spare, counts = total - most - (number_of - 1), [1] * (number_of - 1)
    while spare > 0:
        free = [i for i in range(number_of - 1) if counts[i] < most]
        mass, left = sum([portions[i] for i in free]), spare
        for i in free:
            more = min(most - counts[i], max(1, left * portions[i] // mass), spare)
            counts[i] = counts[i] + more
            spare = spare - more
    return np.array([most] + counts)


def uneven(own_key, count, total, most, skew):
    if count == 2:
        one = jax.random.randint(own_key, (), max(1, total - most), min(most, total - 1) + 1)
        return jnp.stack([one, total - one])
    tallies = jnp.asarray(length_profile(count, total, most, skew), jnp.int32)
    couples = (count - 1) // 2
    donor, taker = tallies[1:1 + 2 * couples:2], tallies[2:2 + 2 * couples:2]
    room = jnp.minimum(donor - 1, most - taker)
    moved = jax.random.randint(jax.random.fold_in(own_key, 1), (couples,), 0, 1 << 20) % (room + 1)
    tallies = tallies.at[1:1 + 2 * couples:2].set(donor - moved).at[2:2 + 2 * couples:2].set(taker + moved)
    return tallies[jax.random.permutation(jax.random.fold_in(own_key, 2), count)]


def gaussian(rng, shape, width, bound, shards=(), held_as=jnp.bfloat16):
    entries = width * jax.random.normal(rng, shape, jnp.float32)
    if shards:
        entries = entries * levels(rng, shape, shards, -0.22, 0.18)
    return jnp.clip(entries, -bound, bound).astype(held_as)


def setup_inputs(seed: int = 0) -> dict:
    streams_of = jax.random.split(jax.random.key(seed), 14)
    return {
        "leaf_right": gaussian(streams_of[0], (RIGHT_SIDES, NSUB * NB), 1.0, 6.0, ((1, 32),), jnp.float32),
        "leaf_inverse": draw_leaf_inverse(jax.random.fold_in(streams_of[13], 71), 0),
        "leaf_link": gaussian(streams_of[2], (NSUB, NB, NB), (4 * NB) ** -0.5, 0.25, ((0, 32),), jnp.float32),
        "leaf_front": gaussian(streams_of[3], (NSUB, NB, NB), (NB * FEEDS) ** -0.5, 0.375, ((0, 32),), jnp.float32),
        "parents": draw_parents(jax.random.fold_in(streams_of[13], 71), 0),
        "front_rows": set_ends(jax.random.randint(streams_of[5], (NSUB,), 0, FBG), jax.random.fold_in(streams_of[5], 1), 0, FBG - 1).astype(jnp.int32),
        "live_blocks": uneven(streams_of[6], DEVS, LIVE_TOTAL, SB, 2).astype(jnp.int32),
        "front_right": gaussian(streams_of[7], (RIGHT_SIDES, GROWS), 1.0, 6.0, ((1, 32),), jnp.float32),
        "front_inverse": draw_front_inverse(jax.random.fold_in(streams_of[13], 71), 0),
        "front_couple": gaussian(streams_of[9], (GROWS, CHAIN_LEVELS * LEVEL_ROWS), GROWS ** -0.5, 0.09375, ((0, 32),), jnp.float32),
        "root_right": gaussian(streams_of[10], (RIGHT_SIDES, CHAIN_LEVELS, LEVEL_ROWS), 1.0, 6.0, ((2, 16),), jnp.float32),
        "root_inverse": draw_root_inverse(jax.random.fold_in(streams_of[13], 71), 0),
        "root_couple": gaussian(streams_of[12], (NPAIR, LEVEL_ROWS, LEVEL_ROWS), (LEVEL_ROWS * CHAIN_LEVELS) ** -0.5, 0.09375, ((1, 16), (2, 2)), jnp.float32),
    }


EXACT_ARITHMETIC = lax.Precision.HIGHEST


def front_table(targets, blocks_front):
    return (targets[:, None] == jnp.arange(blocks_front, dtype=jnp.int32)[None, :]).astype(jnp.float32)


def piece_forward(right_side, inverse, linked, parents, live_count, upper_bound):
    total_blocks = inverse.shape[0]

    def advance(member, loop_state):
        pending, solved = loop_state
        is_alive = member < live_count
        residual = lax.dynamic_index_in_dim(right_side, member, 1, False) - lax.dynamic_index_in_dim(pending, member, 1, False)
        solved_block = jnp.where(is_alive, jnp.dot(residual, inverse[member], precision=EXACT_ARITHMETIC), 0.0)
        solved = lax.dynamic_update_index_in_dim(solved, solved_block, member, 1)
        target = parents[member]
        target_slot = jnp.minimum(target, total_blocks - 1)
        update = jnp.where(target < live_count, jnp.dot(solved_block, linked[member], precision=EXACT_ARITHMETIC), 0.0)
        current = lax.dynamic_index_in_dim(pending, target_slot, 1, False)
        pending = lax.dynamic_update_index_in_dim(pending, current + update, target_slot, 1)
        return pending, solved

    empty_state = jnp.zeros_like(right_side)
    return lax.fori_loop(0, upper_bound, advance, (empty_state, empty_state))[1]


def piece_backward(base_terms, inverse, linked, parents, live_count, upper_bound):
    total_blocks = inverse.shape[0]

    def retreat(turn_index, solved):
        member = upper_bound - 1 - turn_index
        is_alive = member < live_count
        target = parents[member]
        target_slot = jnp.minimum(target, total_blocks - 1)
        parent_value = lax.dynamic_index_in_dim(solved, target_slot, 1, False)
        carried = jnp.where(target < live_count, jnp.einsum("rn,mn->rm", parent_value, linked[member], precision=EXACT_ARITHMETIC), 0.0)
        residual = lax.dynamic_index_in_dim(base_terms, member, 1, False) - carried
        solved_block = jnp.where(is_alive, jnp.einsum("rn,mn->rm", residual, inverse[member], precision=EXACT_ARITHMETIC), 0.0)
        return lax.dynamic_update_index_in_dim(solved, solved_block, member, 1)

    return lax.fori_loop(0, upper_bound, retreat, jnp.zeros_like(base_terms))


def front_update(solved, coupled, targets, blocks_front):
    contrib = jnp.einsum("rkn,knm->rkm", solved, coupled, precision=EXACT_ARITHMETIC)
    table = front_table(targets, blocks_front)
    placed = jnp.einsum("rkm,kf->rfm", contrib, table, precision=EXACT_ARITHMETIC)
    return placed.reshape(solved.shape[0], -1)


def front_back(front_values, coupled, targets, blocks_front):
    table = front_table(targets, blocks_front)
    grouped = front_values.reshape(front_values.shape[0], blocks_front, -1)
    picked = jnp.einsum("rfn,kf->rkn", grouped, table, precision=EXACT_ARITHMETIC)
    return jnp.einsum("rkn,kmn->rkm", picked, coupled, precision=EXACT_ARITHMETIC)


def reference(leaf_right, leaf_inverse, leaf_link, leaf_front, parents, front_rows, live_blocks, front_right, front_inverse, front_couple, root_right, root_inverse, root_couple):
    right_pieces = leaf_right.reshape(RIGHT_SIDES, DEVS, SB, NB)
    inverse_pieces = leaf_inverse.reshape(DEVS, SB, NB, NB)
    link_pieces = leaf_link.reshape(DEVS, SB, NB, NB)
    front_pieces = leaf_front.reshape(DEVS, SB, NB, NB)
    parent_pieces = parents.reshape(DEVS, SB)
    target_pieces = front_rows.reshape(DEVS, SB)

    def forward_one(right_side, inverse, linked, coupled, parent_row, target_row, live_count):
        solved = piece_forward(right_side, inverse, linked, parent_row, live_count, SB)
        return solved, front_update(solved, coupled, target_row, FBG)

    solved_all, updates = jax.vmap(forward_one, in_axes=(1, 0, 0, 0, 0, 0, 0))(right_pieces, inverse_pieces, link_pieces, front_pieces, parent_pieces, target_pieces, live_blocks)
    group_updates = jnp.sum(updates.reshape(N_GRP, N_DEV, RIGHT_SIDES, FG), axis=1)
    group_right = jnp.transpose(front_right.reshape(RIGHT_SIDES, N_GRP, FG), (1, 0, 2))
    group_inverse = front_inverse.reshape(N_GRP, FG, FG)
    group_coupling_block = front_couple.reshape(N_GRP, FG, CHAIN_LEVELS * LEVEL_ROWS)
    forward_front_sweep = jnp.einsum("grf,gfh->grh", group_right - group_updates, group_inverse, precision=EXACT_ARITHMETIC)
    raised_values = jnp.einsum("dpl,dlt->pt", forward_front_sweep, group_coupling_block, precision=EXACT_ARITHMETIC).reshape(RIGHT_SIDES, CHAIN_LEVELS, LEVEL_ROWS)

    forward_values = [None] * CHAIN_LEVELS
    for height in reversed(range(CHAIN_LEVELS)):
        residual = root_right[:, height] - raised_values[:, height]
        for upper_level in range(height + 1, CHAIN_LEVELS):
            residual = residual - jnp.einsum("rj,ij->ri", forward_values[upper_level], root_couple[upper_level * (upper_level - 1) // 2 + height], precision=EXACT_ARITHMETIC)
        forward_values[height] = jnp.dot(residual, root_inverse[height], precision=EXACT_ARITHMETIC)
    back_values = [None] * CHAIN_LEVELS
    for height in range(CHAIN_LEVELS):
        residual = forward_values[height]
        for lower_level in range(height):
            residual = residual - jnp.dot(back_values[lower_level], root_couple[height * (height - 1) // 2 + lower_level], precision=EXACT_ARITHMETIC)
        back_values[height] = jnp.einsum("rj,ij->ri", residual, root_inverse[height], precision=EXACT_ARITHMETIC)
    root_solution = jnp.stack(back_values, 1)

    flattened_root = root_solution.reshape(RIGHT_SIDES, CHAIN_LEVELS * LEVEL_ROWS)
    backward_remainder = forward_front_sweep - jnp.einsum("sv,dmv->dsm", flattened_root, group_coupling_block, precision=EXACT_ARITHMETIC)
    front_values = jnp.einsum("grh,gfh->grf", backward_remainder, group_inverse, precision=EXACT_ARITHMETIC)
    front_solution = jnp.transpose(front_values, (1, 0, 2)).reshape(RIGHT_SIDES, N_GRP * FG)
    piece_fronts = jnp.repeat(front_values, N_DEV, axis=0)

    def backward_one(solved, inverse, linked, coupled, parent_row, target_row, live_count, front_piece):
        base_terms = solved - front_back(front_piece, coupled, target_row, FBG)
        return piece_backward(base_terms, inverse, linked, parent_row, live_count, SB)

    leaf_all = jax.vmap(backward_one)(solved_all, inverse_pieces, link_pieces, front_pieces, parent_pieces, target_pieces, live_blocks, piece_fronts)
    leaf_solution = jnp.transpose(leaf_all, (1, 0, 2, 3)).reshape(RIGHT_SIDES, NSUB * NB)
    return leaf_solution, front_solution, root_solution
```

```python
import functools

import jax
import jax.numpy as jnp
from jax import lax
from jax.experimental import pallas as pl
from jax.experimental.pallas import tpu as pltpu
from jax.sharding import PartitionSpec as P

MESH = pl.DeviceIdType.MESH
ROW_TILE = 8
F32 = jnp.float32
BF16 = jnp.bfloat16

(
    FRONT_SUM,
    FRONT_SOLVE,
    RAISE_TOP,
    RAISE_LOW,
    RAISE_TOP_GRP,
    RAISE_LOW_GRP,
    TOP_SUM,
    TOP_SHARE,
    PUSH_GRP,
    LOW_SUM,
    LOW_SHARE,
    LOW_BACK_GRP,
    CORRECT_SUM,
    CORRECT_SHARE,
    LOW_ALL,
    TOP_BACK_GRP,
    TOP_ALL,
    REMAINDER_ALL,
    FRONT_ALL,
    PHASES,
) = range(20)


def split(values):
    high = values.astype(BF16)
    return high, (values - high.astype(F32)).astype(BF16)


def product(left, high, low, transposed=False):
    rows = left.shape[0]
    left_high, left_low = split(left)
    contract = (((1,), (1 if transposed else 0,)), ((), ()))
    both = lax.dot_general(
        jnp.concatenate([left_high, left_low], 0), high, contract, preferred_element_type=F32
    )
    rest = lax.dot_general(left_high, low, contract, preferred_element_type=F32)
    return both[:rows] + both[rows:] + rest


def kernel(
    groups,
    devs,
    parents,
    targets,
    live_blocks,
    root_right,
    leaf_right_hbm,
    leaf_inverse_hbm,
    leaf_link_hbm,
    leaf_front_hbm,
    front_right_hbm,
    front_inverse_hbm,
    front_couple_hbm,
    root_inverse_hbm,
    root_couple_hbm,
    leaf_out,
    front_out,
    root_out,
    leaf_right,
    leaf_inverse,
    leaf_link,
    leaf_front,
    front_right,
    front_inverse,
    front_couple,
    root_inverse,
    root_couple,
    fi_high,
    fi_low,
    fc_high,
    fc_low,
    ri_high,
    ri_low,
    rc_high,
    rc_low,
    solved,
    front_sum_part,
    front_sum_got,
    front_solve_part,
    front_solve_got,
    raise_top_part,
    raise_top_got,
    raise_low_part,
    raise_low_got,
    top_part,
    top_got,
    top_share,
    low_part,
    low_got,
    low_share,
    correct_part,
    correct_got,
    correct_share,
    raise_top_grp,
    raise_low_grp,
    push_grp,
    low_back_grp,
    top_back_grp,
    low_all,
    top_all,
    remainder_all,
    front_all,
    load_sem,
    send_sem,
    recv_sem,
):
    group = lax.axis_index("grp")
    me = lax.axis_index("dev")
    columns = leaf_right.shape[0]
    blocks_here, width = leaf_inverse.shape[0], leaf_inverse.shape[1]
    front_order = front_inverse.shape[1]
    blocks_front = front_order // width
    front_part = front_right.shape[1]
    level_rows = front_couple.shape[1] // 2
    level_part = level_rows // devs
    level_columns = root_inverse.shape[2]
    row_tiles = columns // ROW_TILE
    piece = top_part.shape[2]

    loads = [
        pltpu.make_async_copy(source, target, load_sem.at[place])
        for place, (source, target) in enumerate(
            (
                (leaf_right_hbm, leaf_right),
                (leaf_inverse_hbm, leaf_inverse),
                (leaf_link_hbm, leaf_link),
                (leaf_front_hbm, leaf_front),
                (front_right_hbm, front_right),
                (front_inverse_hbm, front_inverse),
                (front_couple_hbm, front_couple),
                (root_inverse_hbm, root_inverse),
                (root_couple_hbm, root_couple),
            )
        )
    ]
    for load in loads:
        load.start()

    barrier = pltpu.get_barrier_semaphore()

    def greet_dev(step, carry):
        pl.semaphore_signal(
            barrier, inc=1, device_id=(group, lax.rem(me + step, devs)), device_id_type=MESH
        )
        return carry

    def greet_grp(step, carry):
        pl.semaphore_signal(
            barrier, inc=1, device_id=(lax.rem(group + step, groups), me), device_id_type=MESH
        )
        return carry

    lax.fori_loop(1, devs, greet_dev, 0)
    lax.fori_loop(1, groups, greet_grp, 0)

    def scatter(phase, part, got):
        def one(step, carry):
            peer = lax.rem(me + step, devs)
            pltpu.make_async_remote_copy(
                src_ref=part.at[peer],
                dst_ref=got.at[step],
                send_sem=send_sem.at[phase],
                recv_sem=recv_sem.at[phase],
                device_id=(group, peer),
                device_id_type=MESH,
            ).start()
            return carry

        lax.fori_loop(1, devs, one, 0)
        got[0] = part[me]

    def share(phase, values, buffer):
        buffer[me] = values

        def one(step, carry):
            pltpu.make_async_remote_copy(
                src_ref=buffer.at[me],
                dst_ref=buffer.at[me],
                send_sem=send_sem.at[phase],
                recv_sem=recv_sem.at[phase],
                device_id=(group, lax.rem(me + step, devs)),
                device_id_type=MESH,
            ).start()
            return carry

        lax.fori_loop(1, devs, one, 0)

    def share_grp(phase, values, buffer):
        buffer[group] = values

        def one(step, carry):
            pltpu.make_async_remote_copy(
                src_ref=buffer.at[group],
                dst_ref=buffer.at[group],
                send_sem=send_sem.at[phase],
                recv_sem=recv_sem.at[phase],
                device_id=(lax.rem(group + step, groups), me),
                device_id_type=MESH,
            ).start()
            return carry

        lax.fori_loop(1, groups, one, 0)

    def settle(semaphore, phase, buffer):
        some = buffer.at[pl.ds(1, buffer.shape[0] - 1)]
        pltpu.make_async_copy(some, some, semaphore.at[phase]).wait()

    def total(phase, buffer):
        settle(recv_sem, phase, buffer)
        result = buffer[0]
        for place in range(1, buffer.shape[0]):
            result = result + buffer[place]
        return result

    def arrived(phase, buffer):
        settle(recv_sem, phase, buffer)
        return jnp.concatenate([buffer[place] for place in range(buffer.shape[0])], 1)

    def split_rows(source, high, low):
        step_rows = 2 * ROW_TILE

        def one(step, carry):
            rows = pl.ds(pl.multiple_of(step * step_rows, step_rows), step_rows)
            high[rows, :], low[rows, :] = split(source[rows, :])
            return carry

        lax.fori_loop(0, source.shape[0] // step_rows, one, 0)

    def spread(left, high, low, start, part, span):
        count = part.shape[0] * span
        chunk = min(count, 512)
        for at in range(0, count, chunk):
            here = product(
                left, high[:, start + at : start + at + chunk], low[:, start + at : start + at + chunk]
            )
            for block in range(chunk // span):
                part[at // span + block] = here[:, block * span : (block + 1) * span]

    def spread_pieces(left, high, low, part):
        here = product(left, high[...], low[...])
        for across in range(devs // row_tiles):
            for down in range(row_tiles):
                part[across * row_tiles + down] = here[
                    down * ROW_TILE : (down + 1) * ROW_TILE, across * piece : (across + 1) * piece
                ]

    def arrived_pieces(phase, buffer):
        settle(recv_sem, phase, buffer)
        return jnp.concatenate(
            [
                jnp.concatenate(
                    [buffer[across * row_tiles + down] for down in range(row_tiles)], 0
                )
                for across in range(devs // row_tiles)
            ],
            1,
        )

    live = live_blocks[0]
    for place in range(4):
        loads[place].wait()
    updates = []
    contributions = []
    for k in range(blocks_here):
        residual = leaf_right[:, k * width : (k + 1) * width]
        for child in range(k):
            residual = residual - jnp.where(parents[child] == k, updates[child], 0.0)
        block = jnp.where(k < live, product(residual, *split(leaf_inverse[k])), 0.0)
        solved[k] = block
        if k < blocks_here - 1:
            updates.append(product(block, *split(leaf_link[k])))
        contributions.append(product(block, *split(leaf_front[k])))
    spans = width // front_part
    for block in range(blocks_front):
        placed = jnp.zeros((columns, width), F32)
        for k in range(blocks_here):
            placed = placed + jnp.where(targets[k] == block, contributions[k], 0.0)
        for within in range(spans):
            front_sum_part[block * spans + within] = placed[
                :, within * front_part : (within + 1) * front_part
            ]

    pl.semaphore_wait(barrier, devs - 1 + groups - 1)
    scatter(FRONT_SUM, front_sum_part, front_sum_got)

    loads[4].wait()
    loads[5].wait()
    split_rows(front_inverse, fi_high, fi_low)
    residual = front_right[...] - total(FRONT_SUM, front_sum_got)
    spread(residual, fi_high, fi_low, 0, front_solve_part, front_part)
    scatter(FRONT_SOLVE, front_solve_part, front_solve_got)
    loads[6].wait()
    split_rows(front_couple, fc_high, fc_low)
    front_forward = total(FRONT_SOLVE, front_solve_got)

    spread(front_forward, fc_high, fc_low, level_rows, raise_top_part, level_part)
    scatter(RAISE_TOP, raise_top_part, raise_top_got)
    spread(front_forward, fc_high, fc_low, 0, raise_low_part, level_part)
    loads[7].wait()
    loads[8].wait()
    for level in range(2):
        split_rows(root_inverse.at[level], ri_high.at[level], ri_low.at[level])
    split_rows(root_couple.at[0], rc_high, rc_low)
    raised_top = total(RAISE_TOP, raise_top_got)
    share_grp(RAISE_TOP_GRP, raised_top, raise_top_grp)
    scatter(RAISE_LOW, raise_low_part, raise_low_got)

    residual = root_right[:, 1, :] - total(RAISE_TOP_GRP, raise_top_grp)
    spread_pieces(residual, ri_high[1], ri_low[1], top_part)
    scatter(TOP_SUM, top_part, top_got)
    share_grp(RAISE_LOW_GRP, total(RAISE_LOW, raise_low_got), raise_low_grp)
    share(TOP_SHARE, total(TOP_SUM, top_got), top_share)
    low_right = root_right[:, 0, :] - total(RAISE_LOW_GRP, raise_low_grp)
    top_forward = arrived_pieces(TOP_SHARE, top_share)

    share_grp(PUSH_GRP, product(top_forward, rc_high[...], rc_low[...], True), push_grp)
    residual = low_right - total(PUSH_GRP, push_grp)
    spread_pieces(residual, ri_high[0], ri_low[0], low_part)
    scatter(LOW_SUM, low_part, low_got)
    share(LOW_SHARE, total(LOW_SUM, low_got), low_share)
    low_forward = arrived_pieces(LOW_SHARE, low_share)

    share_grp(LOW_BACK_GRP, product(low_forward, ri_high[0], ri_low[0], True), low_back_grp)
    low_solution = total(LOW_BACK_GRP, low_back_grp)
    root_out[:, 0, :] = low_solution
    spread_pieces(low_solution, rc_high[...], rc_low[...], correct_part)
    scatter(CORRECT_SUM, correct_part, correct_got)
    share(LOW_ALL, low_solution, low_all)
    share(CORRECT_SHARE, total(CORRECT_SUM, correct_got), correct_share)
    lifted = product(
        arrived(LOW_ALL, low_all), fc_high[:, :level_rows], fc_low[:, :level_rows], True
    )
    residual = top_forward - arrived_pieces(CORRECT_SHARE, correct_share)
    share_grp(TOP_BACK_GRP, product(residual, ri_high[1], ri_low[1], True), top_back_grp)
    top_solution = total(TOP_BACK_GRP, top_back_grp)
    share(TOP_ALL, top_solution, top_all)
    root_out[:, 1, :] = top_solution

    lifted = lifted + product(
        arrived(TOP_ALL, top_all), fc_high[:, level_rows:], fc_low[:, level_rows:], True
    )
    share(REMAINDER_ALL, front_forward - lifted, remainder_all)
    remainder = arrived(REMAINDER_ALL, remainder_all)
    share(FRONT_ALL, product(remainder, fi_high[...], fi_low[...], True), front_all)
    front_out[...] = arrived(FRONT_ALL, front_all)

    solutions = [None] * blocks_here
    for k in reversed(range(blocks_here)):
        picked = jnp.zeros((columns, width), F32)
        for block in range(blocks_front):
            picked = picked + jnp.where(
                targets[k] == block, front_out[:, block * width : (block + 1) * width], 0.0
            )
        residual = solved[k] - product(picked, *split(leaf_front[k]), True)
        if k < blocks_here - 1:
            above = jnp.zeros((columns, width), F32)
            for other in range(k + 1, blocks_here):
                above = above + jnp.where(parents[k] == other, solutions[other], 0.0)
            residual = residual - product(above, *split(leaf_link[k]), True)
        solutions[k] = jnp.where(k < live, product(residual, *split(leaf_inverse[k]), True), 0.0)
        leaf_out[:, k * width : (k + 1) * width] = solutions[k]

    for phase, buffer in (
        (FRONT_SUM, front_sum_part),
        (FRONT_SOLVE, front_solve_part),
        (RAISE_TOP, raise_top_part),
        (RAISE_LOW, raise_low_part),
        (RAISE_TOP_GRP, raise_top_grp),
        (RAISE_LOW_GRP, raise_low_grp),
        (TOP_SUM, top_part),
        (TOP_SHARE, top_share),
        (PUSH_GRP, push_grp),
        (LOW_SUM, low_part),
        (LOW_SHARE, low_share),
        (LOW_BACK_GRP, low_back_grp),
        (CORRECT_SUM, correct_part),
        (CORRECT_SHARE, correct_share),
        (LOW_ALL, low_all),
        (TOP_BACK_GRP, top_back_grp),
        (TOP_ALL, top_all),
        (REMAINDER_ALL, remainder_all),
        (FRONT_ALL, front_all),
    ):
        settle(send_sem, phase, buffer)


def body(
    groups,
    devs,
    leaf_right,
    leaf_inverse,
    leaf_link,
    leaf_front,
    parents,
    front_rows,
    live_blocks,
    front_right,
    front_inverse,
    front_couple,
    root_right,
    root_inverse,
    root_couple,
):
    columns = leaf_right.shape[0]
    front_part = front_right.shape[1]
    level_part = root_right.shape[2]
    level_columns = root_inverse.shape[2]
    row_tiles = columns // ROW_TILE
    piece = level_columns * row_tiles // devs
    loaded = (
        leaf_right,
        leaf_inverse,
        leaf_link,
        leaf_front,
        front_right,
        front_inverse,
        front_couple,
        root_inverse,
        root_couple,
    )
    in_halves = (front_inverse, front_couple, root_inverse, root_couple[0])
    front_blocks = pltpu.VMEM((devs, columns, front_part), F32)
    level_blocks = pltpu.VMEM((devs, columns, level_part), F32)
    pieces = pltpu.VMEM((devs, ROW_TILE, piece), F32)
    grp_blocks = pltpu.VMEM((groups, columns, level_part), F32)
    vmem = pl.BlockSpec(memory_space=pltpu.VMEM)
    smem = pl.BlockSpec(memory_space=pltpu.SMEM)
    anywhere = pl.BlockSpec(memory_space=pl.ANY)
    return pl.pallas_call(
        functools.partial(kernel, groups, devs),
        out_shape=(
            jax.ShapeDtypeStruct(leaf_right.shape, F32),
            jax.ShapeDtypeStruct((columns, front_part * devs), F32),
            jax.ShapeDtypeStruct(root_right.shape, F32),
        ),
        in_specs=[smem] * 3 + [vmem] + [anywhere] * len(loaded),
        out_specs=(vmem, vmem, vmem),
        scratch_shapes=[pltpu.VMEM(array.shape, F32) for array in loaded]
        + [pltpu.VMEM(array.shape, BF16) for array in in_halves for _ in range(2)]
        + [pltpu.VMEM((leaf_inverse.shape[0], columns, leaf_inverse.shape[1]), F32)]
        + [front_blocks] * 4
        + [level_blocks] * 4
        + [pieces] * 9
        + [grp_blocks] * 5
        + [level_blocks] * 2
        + [front_blocks] * 2
        + [
            pltpu.SemaphoreType.DMA((len(loaded),)),
            pltpu.SemaphoreType.DMA((PHASES,)),
            pltpu.SemaphoreType.DMA((PHASES,)),
        ],
        compiler_params=pltpu.CompilerParams(
            collective_id=0, has_side_effects=True, vmem_limit_bytes=48 * 1024 * 1024
        ),
        name="block_solves",
    )(parents, front_rows, live_blocks, root_right, *loaded)


def solution(mesh):
    in_specs = (
        P(None, ("grp", "dev")),
        P(("grp", "dev"), None, None),
        P(("grp", "dev"), None, None),
        P(("grp", "dev"), None, None),
        P(("grp", "dev")),
        P(("grp", "dev")),
        P(("grp", "dev")),
        P(None, ("grp", "dev")),
        P(("grp", "dev"), None),
        P(("grp", "dev"), None),
        P(None, None, "dev"),
        P(None, "dev", "grp"),
        P(None, "dev", "grp"),
    )
    out_specs = (P(None, ("grp", "dev")), P(None, "grp"), P(None, None, "dev"))
    return jax.shard_map(
        functools.partial(body, mesh.shape["grp"], mesh.shape["dev"]),
        mesh=mesh,
        in_specs=in_specs,
        out_specs=out_specs,
        check_vma=False,
    )
```

```python
import functools

import jax
import jax.numpy as jnp
from jax import lax
from jax.experimental import pallas as pl
from jax.experimental.pallas import tpu as pltpu
from jax.sharding import PartitionSpec as P

MESH = pl.DeviceIdType.MESH
ROW_TILE = 8
F32 = jnp.float32
BF16 = jnp.bfloat16

(
    FRONT_SUM,
    FRONT_SOLVE,
    RAISE_TOP,
    RAISE_LOW,
    RAISE_TOP_GRP,
    RAISE_LOW_GRP,
    TOP_SUM,
    TOP_SHARE,
    PUSH_GRP,
    LOW_SUM,
    LOW_SHARE,
    LOW_BACK_GRP,
    CORRECT_SUM,
    CORRECT_SHARE,
    LOW_ALL,
    TOP_BACK_GRP,
    TOP_ALL,
    REMAINDER_ALL,
    FRONT_ALL,
    PHASES,
) = range(20)


def split(values):
    high = values.astype(BF16)
    return high, (values - high.astype(F32)).astype(BF16)


def product(left, high, low, transposed=False):
    rows = left.shape[0]
    left_high, left_low = split(left)
    contract = (((1,), (1 if transposed else 0,)), ((), ()))
    both = lax.dot_general(
        jnp.concatenate([left_high, left_low], 0), high, contract, preferred_element_type=F32
    )
    rest = lax.dot_general(left_high, low, contract, preferred_element_type=F32)
    return both[:rows] + both[rows:] + rest


def kernel(
    groups,
    devs,
    parents,
    targets,
    live_blocks,
    root_right,
    leaf_right_hbm,
    leaf_inverse_hbm,
    leaf_link_hbm,
    leaf_front_hbm,
    front_right_hbm,
    front_inverse_hbm,
    front_couple_hbm,
    root_inverse_hbm,
    root_couple_hbm,
    leaf_out,
    front_out,
    root_out,
    leaf_right,
    leaf_inverse,
    leaf_link,
    leaf_front,
    front_right,
    front_inverse,
    front_couple,
    root_inverse,
    root_couple,
    fi_high,
    fi_low,
    fc_high,
    fc_low,
    ri_high,
    ri_low,
    rc_high,
    rc_low,
    solved,
    front_sum_part,
    front_solve_part,
    front_sum_pair,
    front_sum_got,
    front_solve_pair,
    front_solve_got,
    raise_top_part,
    raise_low_part,
    raise_top_pair,
    raise_top_got,
    raise_low_pair,
    raise_low_got,
    top_part,
    low_part,
    correct_part,
    top_share,
    low_share,
    correct_share,
    top_pair,
    top_got,
    low_pair,
    low_got,
    correct_pair,
    correct_got,
    raise_top_grp,
    raise_low_grp,
    push_grp,
    low_back_grp,
    top_back_grp,
    low_all,
    top_all,
    remainder_all,
    front_all,
    load_sem,
    send_sem,
    recv_sem,
    pair_send_sem,
    pair_recv_sem,
):
    group = lax.axis_index("grp")
    me = lax.axis_index("dev")
    chips = devs // 2
    chip = me // 2
    core = lax.rem(me, 2)
    other = 1 - core
    sibling = (group, chip * 2 + other)
    columns = leaf_right.shape[0]
    blocks_here, width = leaf_inverse.shape[0], leaf_inverse.shape[1]
    blocks_front = front_inverse.shape[1] // width
    front_part = front_right.shape[1]
    level_rows = front_couple.shape[1] // 2
    row_tiles = columns // ROW_TILE
    piece = top_part.shape[3]

    def chip_peer(step):
        return (group, lax.rem(chip + step, chips) * 2 + core)

    def grp_peer(step):
        return (lax.rem(group + step, groups), me)

    loads = [
        pltpu.make_async_copy(source, target, load_sem.at[place])
        for place, (source, target) in enumerate(
            (
                (leaf_right_hbm, leaf_right),
                (leaf_inverse_hbm, leaf_inverse),
                (leaf_link_hbm, leaf_link),
                (leaf_front_hbm, leaf_front),
                (front_right_hbm, front_right),
                (front_inverse_hbm, front_inverse),
                (front_couple_hbm, front_couple),
                (root_inverse_hbm, root_inverse),
                (root_couple_hbm, root_couple),
            )
        )
    ]
    for load in loads:
        load.start()

    barrier = pltpu.get_barrier_semaphore()

    def greet(device):
        pl.semaphore_signal(barrier, inc=1, device_id=device, device_id_type=MESH)

    greet(sibling)
    for step in range(1, chips):
        greet(chip_peer(step))
    for step in range(1, groups):
        greet(grp_peer(step))

    def send(source, target, device, phase):
        pltpu.make_async_remote_copy(
            src_ref=source,
            dst_ref=target,
            send_sem=send_sem.at[phase],
            recv_sem=recv_sem.at[phase],
            device_id=device,
            device_id_type=MESH,
        ).start()

    def send_pair(source, target, phase):
        pltpu.make_async_remote_copy(
            src_ref=source,
            dst_ref=target,
            send_sem=pair_send_sem.at[phase],
            recv_sem=pair_recv_sem.at[phase],
            device_id=sibling,
            device_id_type=MESH,
        ).start()

    def settle(semaphore, some):
        pltpu.make_async_copy(some, some, semaphore).wait()

    def pair_sum(phase, part, pair, fill):
        fill(other, part.at[other])
        send_pair(part.at[other], pair, phase)
        fill(core, part.at[core])

    def chip_send(phase, part, got):
        for step in range(1, chips):
            peer = lax.rem(chip + step, chips)
            send(part.at[core, peer], got.at[step], chip_peer(step), phase)

    def pair_done(phase, part, pair):
        settle(pair_recv_sem.at[phase], pair)
        for place in range(chips):
            part[core, place] = part[core, place] + pair[place]

    def total(phase, part, got):
        result = part[core, chip]
        settle(recv_sem.at[phase], got.at[pl.ds(1, chips - 1)])
        for place in range(1, chips):
            result = result + got[place]
        return result

    def share(phase, values, buffer):
        buffer[core, chip] = values
        for step in range(1, chips):
            send(buffer.at[core, chip], buffer.at[core, chip], chip_peer(step), phase)

    def share_pair(phase, buffer):
        settle(recv_sem.at[phase], buffer.at[0, pl.ds(1, chips - 1)])
        send_pair(buffer.at[core], buffer.at[core], phase)

    def pair_arrived(phase, buffer):
        settle(pair_recv_sem.at[phase], buffer.at[0])

    def share_grp(phase, values, buffer):
        buffer[group] = values
        for step in range(1, groups):
            send(buffer.at[group], buffer.at[group], grp_peer(step), phase)

    def total_grp(phase, buffer):
        settle(recv_sem.at[phase], buffer.at[pl.ds(1, groups - 1)])
        result = buffer[0]
        for place in range(1, groups):
            result = result + buffer[place]
        return result

    def whole(buffer, half):
        return jnp.concatenate([buffer[half, place] for place in range(chips)], 1)

    def whole_pieces(buffer, half):
        return jnp.concatenate(
            [
                jnp.concatenate(
                    [buffer[half, across * row_tiles + down] for down in range(row_tiles)], 0
                )
                for across in range(chips // row_tiles)
            ],
            1,
        )

    def split_rows(source, high, low, span, column=0):
        step_rows = 2 * ROW_TILE
        half = high.shape[2]

        def one(step, carry):
            rows = pl.ds(pl.multiple_of(step * step_rows, step_rows), step_rows)
            for at in range(0, 2 * half, span):
                parity, place = (at // span) % 2, at // span // 2 * span
                upper, lower = split(source[rows, column + at : column + at + span])
                high[parity, rows, place : place + span] = upper
                low[parity, rows, place : place + span] = lower
            return carry

        lax.fori_loop(0, source.shape[0] // step_rows, one, 0)

    def fill_blocks(left, high, low):
        def fill(half, part):
            count, span = part.shape[0], part.shape[2]
            chunk = min(count * span, 512)
            for at in range(0, count * span, chunk):
                here = product(left, high[half, :, at : at + chunk], low[half, :, at : at + chunk])
                for block in range(chunk // span):
                    part[at // span + block] = here[:, block * span : (block + 1) * span]

        return fill

    def fill_pieces(left, high, low):
        def fill(half, part):
            here = product(left, high[half], low[half])
            for across in range(chips // row_tiles):
                for down in range(row_tiles):
                    part[across * row_tiles + down] = here[
                        down * ROW_TILE : (down + 1) * ROW_TILE,
                        across * piece : (across + 1) * piece,
                    ]

        return fill

    def gathered_product(phase, buffer, assemble, high, low):
        share_pair(phase, buffer)
        result = product(assemble(buffer, core), high[core], low[core], True)
        pair_arrived(phase, buffer)
        return result + product(assemble(buffer, other), high[other], low[other], True)

    live = live_blocks[0]
    for place in range(4):
        loads[place].wait()
    updates = []
    contributions = []
    for k in range(blocks_here):
        residual = leaf_right[:, k * width : (k + 1) * width]
        for child in range(k):
            residual = residual - jnp.where(parents[child] == k, updates[child], 0.0)
        block = jnp.where(k < live, product(residual, *split(leaf_inverse[k])), 0.0)
        solved[k] = block
        if k < blocks_here - 1:
            updates.append(product(block, *split(leaf_link[k])))
        contributions.append(product(block, *split(leaf_front[k])))
    spans = width // front_part
    for block in range(blocks_front):
        placed = jnp.zeros((columns, width), F32)
        for k in range(blocks_here):
            placed = placed + jnp.where(targets[k] == block, contributions[k], 0.0)
        for within in range(spans):
            owner = block * spans + within
            front_sum_part[owner % 2, owner // 2] = placed[
                :, within * front_part : (within + 1) * front_part
            ]

    pl.semaphore_wait(barrier, chips + groups - 1)
    send_pair(front_sum_part.at[other], front_sum_pair, FRONT_SUM)
    loads[4].wait()
    loads[5].wait()
    pair_done(FRONT_SUM, front_sum_part, front_sum_pair)
    chip_send(FRONT_SUM, front_sum_part, front_sum_got)

    split_rows(front_inverse, fi_high, fi_low, front_part)
    residual = front_right[...] - total(FRONT_SUM, front_sum_part, front_sum_got)
    pair_sum(FRONT_SOLVE, front_solve_part, front_solve_pair, fill_blocks(residual, fi_high, fi_low))
    pair_done(FRONT_SOLVE, front_solve_part, front_solve_pair)
    chip_send(FRONT_SOLVE, front_solve_part, front_solve_got)
    loads[6].wait()
    level_part = level_rows // devs
    for level in range(2):
        split_rows(
            front_couple, fc_high.at[level], fc_low.at[level], level_part, level * level_rows
        )
    front_forward = total(FRONT_SOLVE, front_solve_part, front_solve_got)

    pair_sum(
        RAISE_TOP,
        raise_top_part,
        raise_top_pair,
        fill_blocks(front_forward, fc_high.at[1], fc_low.at[1]),
    )
    pair_done(RAISE_TOP, raise_top_part, raise_top_pair)
    chip_send(RAISE_TOP, raise_top_part, raise_top_got)
    pair_sum(
        RAISE_LOW,
        raise_low_part,
        raise_low_pair,
        fill_blocks(front_forward, fc_high.at[0], fc_low.at[0]),
    )
    loads[7].wait()
    loads[8].wait()
    half = root_inverse.shape[2] // 2
    for level in (1, 0):
        split_rows(root_inverse.at[level], ri_high.at[level], ri_low.at[level], half)
    split_rows(root_couple.at[0], rc_high, rc_low, half)
    pair_done(RAISE_LOW, raise_low_part, raise_low_pair)
    raised_top = total(RAISE_TOP, raise_top_part, raise_top_got)
    share_grp(RAISE_TOP_GRP, raised_top, raise_top_grp)
    chip_send(RAISE_LOW, raise_low_part, raise_low_got)

    residual = root_right[:, 1, :] - total_grp(RAISE_TOP_GRP, raise_top_grp)
    pair_sum(TOP_SUM, top_part, top_pair, fill_pieces(residual, ri_high.at[1], ri_low.at[1]))
    pair_done(TOP_SUM, top_part, top_pair)
    chip_send(TOP_SUM, top_part, top_got)
    share_grp(RAISE_LOW_GRP, total(RAISE_LOW, raise_low_part, raise_low_got), raise_low_grp)
    share(TOP_SHARE, total(TOP_SUM, top_part, top_got), top_share)
    low_right = root_right[:, 0, :] - total_grp(RAISE_LOW_GRP, raise_low_grp)

    pushed = gathered_product(TOP_SHARE, top_share, whole_pieces, rc_high, rc_low)
    share_grp(PUSH_GRP, pushed, push_grp)
    residual = low_right - total_grp(PUSH_GRP, push_grp)
    pair_sum(LOW_SUM, low_part, low_pair, fill_pieces(residual, ri_high.at[0], ri_low.at[0]))
    pair_done(LOW_SUM, low_part, low_pair)
    chip_send(LOW_SUM, low_part, low_got)
    share(LOW_SHARE, total(LOW_SUM, low_part, low_got), low_share)

    back = gathered_product(LOW_SHARE, low_share, whole_pieces, ri_high.at[0], ri_low.at[0])
    share_grp(LOW_BACK_GRP, back, low_back_grp)
    low_solution = total_grp(LOW_BACK_GRP, low_back_grp)
    pair_sum(CORRECT_SUM, correct_part, correct_pair, fill_pieces(low_solution, rc_high, rc_low))
    pair_done(CORRECT_SUM, correct_part, correct_pair)
    chip_send(CORRECT_SUM, correct_part, correct_got)
    share(LOW_ALL, low_solution, low_all)
    root_out[:, 0, :] = low_solution
    share(CORRECT_SHARE, total(CORRECT_SUM, correct_part, correct_got), correct_share)
    lifted = gathered_product(LOW_ALL, low_all, whole, fc_high.at[0], fc_low.at[0])

    def corrected(buffer, side):
        return whole_pieces(top_share, side) - whole_pieces(buffer, side)

    back = gathered_product(CORRECT_SHARE, correct_share, corrected, ri_high.at[1], ri_low.at[1])
    share_grp(TOP_BACK_GRP, back, top_back_grp)
    top_solution = total_grp(TOP_BACK_GRP, top_back_grp)
    share(TOP_ALL, top_solution, top_all)
    root_out[:, 1, :] = top_solution

    lifted = lifted + gathered_product(TOP_ALL, top_all, whole, fc_high.at[1], fc_low.at[1])
    share(REMAINDER_ALL, front_forward - lifted, remainder_all)
    share(
        FRONT_ALL, gathered_product(REMAINDER_ALL, remainder_all, whole, fi_high, fi_low), front_all
    )
    share_pair(FRONT_ALL, front_all)
    pair_arrived(FRONT_ALL, front_all)
    for owner in range(devs):
        front_out[:, owner * front_part : (owner + 1) * front_part] = front_all[
            owner % 2, owner // 2
        ]

    solutions = [None] * blocks_here
    for k in reversed(range(blocks_here)):
        picked = jnp.zeros((columns, width), F32)
        for block in range(blocks_front):
            picked = picked + jnp.where(
                targets[k] == block, front_out[:, block * width : (block + 1) * width], 0.0
            )
        residual = solved[k] - product(picked, *split(leaf_front[k]), True)
        if k < blocks_here - 1:
            above = jnp.zeros((columns, width), F32)
            for upper in range(k + 1, blocks_here):
                above = above + jnp.where(parents[k] == upper, solutions[upper], 0.0)
            residual = residual - product(above, *split(leaf_link[k]), True)
        solutions[k] = jnp.where(k < live, product(residual, *split(leaf_inverse[k]), True), 0.0)
        leaf_out[:, k * width : (k + 1) * width] = solutions[k]

    for phase, buffer in (
        (FRONT_SUM, front_sum_part),
        (FRONT_SOLVE, front_solve_part),
        (RAISE_TOP, raise_top_part),
        (RAISE_LOW, raise_low_part),
        (TOP_SUM, top_part),
        (TOP_SHARE, top_share),
        (LOW_SUM, low_part),
        (LOW_SHARE, low_share),
        (CORRECT_SUM, correct_part),
        (CORRECT_SHARE, correct_share),
        (LOW_ALL, low_all),
        (TOP_ALL, top_all),
        (REMAINDER_ALL, remainder_all),
        (FRONT_ALL, front_all),
    ):
        settle(send_sem.at[phase], buffer.at[0, pl.ds(1, chips - 1)])
        settle(pair_send_sem.at[phase], buffer.at[0])
    for phase, buffer in (
        (RAISE_TOP_GRP, raise_top_grp),
        (RAISE_LOW_GRP, raise_low_grp),
        (PUSH_GRP, push_grp),
        (LOW_BACK_GRP, low_back_grp),
        (TOP_BACK_GRP, top_back_grp),
    ):
        settle(send_sem.at[phase], buffer.at[pl.ds(1, groups - 1)])


def body(
    groups,
    devs,
    leaf_right,
    leaf_inverse,
    leaf_link,
    leaf_front,
    parents,
    front_rows,
    live_blocks,
    front_right,
    front_inverse,
    front_couple,
    root_right,
    root_inverse,
    root_couple,
):
    columns = leaf_right.shape[0]
    front_part = front_right.shape[1]
    level_part = root_right.shape[2]
    level_columns = root_inverse.shape[2]
    row_tiles = columns // ROW_TILE
    piece = level_columns // 2 * row_tiles // (devs // 2)
    loaded = (
        leaf_right,
        leaf_inverse,
        leaf_link,
        leaf_front,
        front_right,
        front_inverse,
        front_couple,
        root_inverse,
        root_couple,
    )
    rows, half = front_inverse.shape[0], front_inverse.shape[1] // 2
    level_half = front_couple.shape[1] // 4
    root_rows, root_half = root_inverse.shape[1], level_columns // 2
    halves = (
        (2, rows, half),
        (2, 2, rows, level_half),
        (2, 2, root_rows, root_half),
        (2, root_rows, root_half),
    )
    chips = devs // 2
    front_full = pltpu.VMEM((2, chips, columns, front_part), F32)
    front_half = pltpu.VMEM((chips, columns, front_part), F32)
    level_full = pltpu.VMEM((2, chips, columns, level_part), F32)
    level_half_blocks = pltpu.VMEM((chips, columns, level_part), F32)
    pieces_full = pltpu.VMEM((2, chips, ROW_TILE, piece), F32)
    pieces_half = pltpu.VMEM((chips, ROW_TILE, piece), F32)
    grp_blocks = pltpu.VMEM((groups, columns, level_part), F32)
    vmem = pl.BlockSpec(memory_space=pltpu.VMEM)
    smem = pl.BlockSpec(memory_space=pltpu.SMEM)
    anywhere = pl.BlockSpec(memory_space=pl.ANY)
    return pl.pallas_call(
        functools.partial(kernel, groups, devs),
        out_shape=(
            jax.ShapeDtypeStruct(leaf_right.shape, F32),
            jax.ShapeDtypeStruct((columns, front_part * devs), F32),
            jax.ShapeDtypeStruct(root_right.shape, F32),
        ),
        in_specs=[smem] * 3 + [vmem] + [anywhere] * len(loaded),
        out_specs=(vmem, vmem, vmem),
        scratch_shapes=[pltpu.VMEM(array.shape, F32) for array in loaded]
        + [pltpu.VMEM(shape, BF16) for shape in halves for _ in range(2)]
        + [pltpu.VMEM((leaf_inverse.shape[0], columns, leaf_inverse.shape[1]), F32)]
        + [front_full] * 2
        + [front_half] * 4
        + [level_full] * 2
        + [level_half_blocks] * 4
        + [pieces_full] * 6
        + [pieces_half] * 6
        + [grp_blocks] * 5
        + [level_full] * 2
        + [front_full] * 2
        + [
            pltpu.SemaphoreType.DMA((len(loaded),)),
        ]
        + [pltpu.SemaphoreType.DMA((PHASES,))] * 4,
        compiler_params=pltpu.CompilerParams(
            collective_id=0, has_side_effects=True, vmem_limit_bytes=62 * 1024 * 1024
        ),
        name="block_solves",
    )(parents, front_rows, live_blocks, root_right, *loaded)


def solution(mesh):
    in_specs = (
        P(None, ("grp", "dev")),
        P(("grp", "dev"), None, None),
        P(("grp", "dev"), None, None),
        P(("grp", "dev"), None, None),
        P(("grp", "dev")),
        P(("grp", "dev")),
        P(("grp", "dev")),
        P(None, ("grp", "dev")),
        P(("grp", "dev"), None),
        P(("grp", "dev"), None),
        P(None, None, "dev"),
        P(None, "dev", "grp"),
        P(None, "dev", "grp"),
    )
    out_specs = (P(None, ("grp", "dev")), P(None, "grp"), P(None, None, "dev"))
    return jax.shard_map(
        functools.partial(body, mesh.shape["grp"], mesh.shape["dev"]),
        mesh=mesh,
        in_specs=in_specs,
        out_specs=out_specs,
        check_vma=False,
    )
```

```python
import functools

import jax
import jax.numpy as jnp
from jax import lax
from jax.experimental import pallas as pl
from jax.experimental.pallas import tpu as pltpu
from jax.sharding import PartitionSpec as P

MESH = pl.DeviceIdType.MESH
ROW_TILE = 8
F32 = jnp.float32
BF16 = jnp.bfloat16

(
    FRONT_SUM,
    FRONT_SOLVE,
    RAISE_TOP,
    RAISE_LOW,
    RAISE_TOP_QUAD,
    RAISE_LOW_QUAD,
    TOP_SUM,
    TOP_SHARE,
    PUSH_QUAD,
    LOW_SUM,
    LOW_SHARE,
    LOW_BACK_QUAD,
    CORRECT_SUM,
    CORRECT_SHARE,
    LOW_ALL,
    TOP_BACK_QUAD,
    TOP_ALL,
    REMAINDER_ALL,
    FRONT_ALL,
    ROOT_SWAP,
    PHASES,
) = range(21)


def split(values):
    high = values.astype(BF16)
    return high, (values - high.astype(F32)).astype(BF16)


def product(left, stacked):
    rows = left.shape[0]
    high, low = split(left)
    both = jnp.concatenate(
        [jnp.concatenate([high, high], 1), jnp.concatenate([low, low], 1)], 0
    )
    result = jnp.dot(both, stacked, preferred_element_type=F32)
    return result[:rows] + result[rows:]


def product_transposed(left, stacked):
    rows, depth = left.shape[0], stacked.shape[0] // 2
    result = lax.dot_general(
        jnp.concatenate(split(left), 0),
        stacked,
        (((1,), (1,)), ((), ())),
        preferred_element_type=F32,
    )
    result = result[:rows] + result[rows:]
    return result[:, :depth] + result[:, depth:]


def stack(values):
    return jnp.concatenate(split(values), 0)


def kernel(
    groups,
    devs,
    parents,
    targets,
    live_blocks,
    root_right,
    leaf_right_hbm,
    leaf_inverse_hbm,
    leaf_link_hbm,
    leaf_front_hbm,
    front_right_hbm,
    front_inverse_hbm,
    front_couple_hbm,
    root_inverse_hbm,
    root_couple_hbm,
    leaf_out,
    front_out,
    root_out,
    leaf_right,
    leaf_inverse,
    leaf_link,
    leaf_front,
    front_right,
    front_inverse,
    front_couple,
    root_halves,
    fi_stacked,
    fc_stacked,
    root_stacked,
    solved,
    front_sum_part,
    front_solve_part,
    front_sum_pair,
    front_sum_got,
    front_solve_pair,
    front_solve_got,
    raise_top_part,
    raise_low_part,
    raise_top_pair,
    raise_top_got,
    raise_low_pair,
    raise_low_got,
    top_part,
    low_part,
    correct_part,
    top_got,
    low_got,
    correct_got,
    top_share,
    low_share,
    correct_share,
    raise_top_quad,
    raise_low_quad,
    push_quad,
    low_back_quad,
    top_back_quad,
    low_all,
    top_all,
    remainder_all,
    front_all,
    load_sem,
    send_sem,
    recv_sem,
    pair_send_sem,
    pair_recv_sem,
):
    group = lax.axis_index("grp")
    me = lax.axis_index("dev")
    chips = devs // 2
    chip = me // 2
    core = lax.rem(me, 2)
    other = 1 - core
    sibling = (group, chip * 2 + other)
    quad = group * 2 + core
    columns = leaf_right.shape[0]
    blocks_here, width = leaf_inverse.shape[0], leaf_inverse.shape[1]
    blocks_front = front_inverse.shape[1] // width
    front_part = front_right.shape[1]
    level_rows = front_couple.shape[1] // 2
    row_tiles = columns // ROW_TILE
    piece = top_part.shape[2]
    half = root_halves.shape[3]
    quads = 2 * groups
    low_inverse, top_inverse, couple = range(3)

    def chip_peer(step):
        return (group, lax.rem(chip + step, chips) * 2 + core)

    def quad_peer(step):
        peer = lax.rem(quad + step, quads)
        return (peer // 2, chip * 2 + lax.rem(peer, 2))

    def half_of(matrix, side):
        columns_of = pl.ds(pl.multiple_of(side * half, half), half)
        if matrix == couple:
            return root_couple_hbm.at[0, :, columns_of]
        return root_inverse_hbm.at[matrix, :, columns_of]

    loads = [
        pltpu.make_async_copy(source, target, load_sem.at[place])
        for place, (source, target) in enumerate(
            (
                (leaf_right_hbm, leaf_right),
                (leaf_inverse_hbm, leaf_inverse),
                (leaf_link_hbm, leaf_link),
                (leaf_front_hbm, leaf_front),
                (front_right_hbm, front_right),
                (front_inverse_hbm, front_inverse),
                (front_couple_hbm, front_couple),
                (half_of(low_inverse, core), root_halves.at[low_inverse, core]),
                (half_of(top_inverse, core), root_halves.at[top_inverse, core]),
                (half_of(couple, core), root_halves.at[couple, core]),
            )
        )
    ]
    for load in loads:
        load.start()

    barrier = pltpu.get_barrier_semaphore()

    def greet(device):
        pl.semaphore_signal(barrier, inc=1, device_id=device, device_id_type=MESH)

    for step in range(1, chips):
        greet(chip_peer(step))
    for step in range(1, quads):
        greet(quad_peer(step))

    def send(source, target, device, phase):
        pltpu.make_async_remote_copy(
            src_ref=source,
            dst_ref=target,
            send_sem=send_sem.at[phase],
            recv_sem=recv_sem.at[phase],
            device_id=device,
            device_id_type=MESH,
        ).start()

    def send_pair(source, target, phase):
        pltpu.make_async_remote_copy(
            src_ref=source,
            dst_ref=target,
            send_sem=pair_send_sem.at[phase],
            recv_sem=pair_recv_sem.at[phase],
            device_id=sibling,
            device_id_type=MESH,
        ).start()

    def settle(semaphore, some):
        pltpu.make_async_copy(some, some, semaphore).wait()

    def pair_sum(phase, part, pair, fill):
        fill(other, part.at[other])
        send_pair(part.at[other], pair, phase)
        fill(core, part.at[core])

    def chip_send(phase, part, got):
        for step in range(1, chips):
            peer = lax.rem(chip + step, chips)
            send(part.at[core, peer], got.at[step], chip_peer(step), phase)

    def pair_done(phase, part, pair):
        settle(pair_recv_sem.at[phase], pair)
        for place in range(chips):
            part[core, place] = part[core, place] + pair[place]

    def total(phase, part, got):
        result = part[core, chip]
        settle(recv_sem.at[phase], got.at[pl.ds(1, chips - 1)])
        for place in range(1, chips):
            result = result + got[place]
        return result

    def share(phase, values, buffer):
        buffer[core, chip] = values
        for step in range(1, chips):
            send(buffer.at[core, chip], buffer.at[core, chip], chip_peer(step), phase)

    def share_pair(phase, buffer):
        settle(recv_sem.at[phase], buffer.at[0, pl.ds(1, chips - 1)])
        send_pair(buffer.at[core], buffer.at[core], phase)

    def pair_arrived(phase, buffer):
        settle(pair_recv_sem.at[phase], buffer.at[0])

    def share_quad(phase, values, buffer):
        buffer[quad] = values
        for step in range(1, quads):
            send(buffer.at[quad], buffer.at[quad], quad_peer(step), phase)

    def quad_wait(phase, buffer):
        settle(recv_sem.at[phase], buffer.at[pl.ds(1, quads - 1)])

    def total_quad(phase, buffer):
        quad_wait(phase, buffer)
        result = buffer[0]
        for place in range(1, quads):
            result = result + buffer[place]
        return result

    def pair_quad(phase, buffer):
        quad_wait(phase, buffer)
        sides = []
        for side in range(2):
            result = buffer[side]
            for place in range(1, groups):
                result = result + buffer[2 * place + side]
            sides.append(result)
        return jnp.concatenate(sides, 1)

    def own_side(values):
        part = values.shape[1] // 2
        return jnp.where(core == 0, values[:, :part], values[:, part:])

    def whole(buffer, side):
        return jnp.concatenate([buffer[side, place] for place in range(chips)], 1)

    def split_rows(source, stacked, span, column=0):
        step_rows = 2 * ROW_TILE
        count = source.shape[0]

        def one(step, carry):
            at_rows = pl.multiple_of(step * step_rows, step_rows)
            rows = pl.ds(at_rows, step_rows)
            rows_low = pl.ds(pl.multiple_of(at_rows + count, step_rows), step_rows)
            for at in range(0, 2 * stacked.shape[2], span):
                parity, place = (at // span) % 2, at // span // 2 * span
                upper, lower = split(source[rows, column + at : column + at + span])
                stacked[parity, rows, place : place + span] = upper
                stacked[parity, rows_low, place : place + span] = lower
            return carry

        lax.fori_loop(0, count // step_rows, one, 0)

    def split_root(matrix):
        step_rows = 2 * ROW_TILE
        count = root_halves.shape[2]

        def one(step, carry):
            at_rows = pl.multiple_of(step * step_rows, step_rows)
            for side in range(2):
                upper, lower = split(root_halves[matrix, side, pl.ds(at_rows, step_rows), :])
                for start, values in ((side, upper), (side + 2, lower)):
                    rows = pl.multiple_of(at_rows + start * count, step_rows)
                    root_stacked[matrix, pl.ds(rows, step_rows), :] = values
            return carry

        lax.fori_loop(0, count // step_rows, one, 0)

    def fill_blocks(left, stacked):
        def fill(side, part):
            count, span = part.shape[0], part.shape[2]
            chunk = min(count * span, 512)
            for at in range(0, count * span, chunk):
                here = product(left, stacked[side, :, at : at + chunk])
                for block in range(chunk // span):
                    part[at // span + block] = here[:, block * span : (block + 1) * span]

        return fill

    def send_pieces(phase, values, part, got):
        for across in range(chips // row_tiles):
            for down in range(row_tiles):
                part[across * row_tiles + down] = values[
                    down * ROW_TILE : (down + 1) * ROW_TILE,
                    across * piece : (across + 1) * piece,
                ]
        for step in range(1, chips):
            send(part.at[lax.rem(chip + step, chips)], got.at[step], chip_peer(step), phase)

    def share_pieces(phase, share_phase, part, got, buffer):
        settle(recv_sem.at[phase], got.at[pl.ds(1, chips - 1)])
        result = part[chip]
        for place in range(1, chips):
            result = result + got[place]
        buffer[chip] = result
        for step in range(1, chips):
            send(buffer.at[chip], buffer.at[chip], chip_peer(step), share_phase)

    def whole_pieces(buffer):
        return jnp.concatenate(
            [
                jnp.concatenate([buffer[across * row_tiles + down] for down in range(row_tiles)], 0)
                for across in range(chips // row_tiles)
            ],
            1,
        )

    def shared_pieces(phase, buffer):
        settle(recv_sem.at[phase], buffer.at[pl.ds(1, chips - 1)])
        return whole_pieces(buffer)

    def half_product(buffer, stacked, side):
        return product_transposed(whole(buffer, side), stacked[side])

    def gathered_product(phase, buffer, stacked):
        share_pair(phase, buffer)
        result = half_product(buffer, stacked, core)
        pair_arrived(phase, buffer)
        return result + half_product(buffer, stacked, other)

    live = live_blocks[0]
    for place in range(4):
        loads[place].wait()
    updates = []
    contributions = []
    for k in range(blocks_here):
        residual = leaf_right[:, k * width : (k + 1) * width]
        for child in range(k):
            residual = residual - jnp.where(parents[child] == k, updates[child], 0.0)
        block = jnp.where(k < live, product(residual, stack(leaf_inverse[k])), 0.0)
        solved[k] = block
        if k < blocks_here - 1:
            updates.append(product(block, stack(leaf_link[k])))
        contributions.append(product(block, stack(leaf_front[k])))
    spans = width // front_part
    for block in range(blocks_front):
        placed = jnp.zeros((columns, width), F32)
        for k in range(blocks_here):
            placed = placed + jnp.where(targets[k] == block, contributions[k], 0.0)
        for within in range(spans):
            owner = block * spans + within
            front_sum_part[owner % 2, owner // 2] = placed[
                :, within * front_part : (within + 1) * front_part
            ]

    pl.semaphore_wait(barrier, chips - 1 + quads - 1)
    send_pair(front_sum_part.at[other], front_sum_pair, FRONT_SUM)
    for matrix in range(3):
        send_pair(half_of(matrix, other), root_halves.at[matrix, core], ROOT_SWAP)
    loads[4].wait()
    loads[5].wait()
    pair_done(FRONT_SUM, front_sum_part, front_sum_pair)
    chip_send(FRONT_SUM, front_sum_part, front_sum_got)

    split_rows(front_inverse, fi_stacked, front_part)
    residual = front_right[...] - total(FRONT_SUM, front_sum_part, front_sum_got)
    pair_sum(FRONT_SOLVE, front_solve_part, front_solve_pair, fill_blocks(residual, fi_stacked))
    pair_done(FRONT_SOLVE, front_solve_part, front_solve_pair)
    chip_send(FRONT_SOLVE, front_solve_part, front_solve_got)
    loads[6].wait()
    level_part = level_rows // devs
    for level in range(2):
        split_rows(front_couple, fc_stacked.at[level], level_part, level * level_rows)
    front_forward = total(FRONT_SOLVE, front_solve_part, front_solve_got)

    pair_sum(
        RAISE_TOP, raise_top_part, raise_top_pair, fill_blocks(front_forward, fc_stacked.at[1])
    )
    pair_done(RAISE_TOP, raise_top_part, raise_top_pair)
    chip_send(RAISE_TOP, raise_top_part, raise_top_got)
    pair_sum(
        RAISE_LOW, raise_low_part, raise_low_pair, fill_blocks(front_forward, fc_stacked.at[0])
    )
    for place in (7, 8, 9):
        loads[place].wait()
    settle(pair_recv_sem.at[ROOT_SWAP], root_halves.at[:, 0])
    for matrix in range(3):
        split_root(matrix)
    pair_done(RAISE_LOW, raise_low_part, raise_low_pair)

    def less_right(level, values):
        return values - jnp.where(group == 0, root_right[:, level, :], 0.0)

    raised_top = total(RAISE_TOP, raise_top_part, raise_top_got)
    share_quad(RAISE_TOP_QUAD, less_right(1, raised_top), raise_top_quad)
    chip_send(RAISE_LOW, raise_low_part, raise_low_got)

    residual = -pair_quad(RAISE_TOP_QUAD, raise_top_quad)
    send_pieces(TOP_SUM, product(residual, root_stacked[top_inverse]), top_part, top_got)
    raised_low = total(RAISE_LOW, raise_low_part, raise_low_got)
    share_quad(RAISE_LOW_QUAD, less_right(0, raised_low), raise_low_quad)
    share_pieces(TOP_SUM, TOP_SHARE, top_part, top_got, top_share)
    low_right = -pair_quad(RAISE_LOW_QUAD, raise_low_quad)

    top_forward = shared_pieces(TOP_SHARE, top_share)
    share_quad(PUSH_QUAD, product_transposed(top_forward, root_stacked[couple]), push_quad)
    residual = low_right - total_quad(PUSH_QUAD, push_quad)
    send_pieces(LOW_SUM, product(residual, root_stacked[low_inverse]), low_part, low_got)
    share_pieces(LOW_SUM, LOW_SHARE, low_part, low_got, low_share)

    low_forward = shared_pieces(LOW_SHARE, low_share)
    back = product_transposed(low_forward, root_stacked[low_inverse])
    share_quad(LOW_BACK_QUAD, back, low_back_quad)
    low_pair = total_quad(LOW_BACK_QUAD, low_back_quad)
    send_pieces(CORRECT_SUM, product(low_pair, root_stacked[couple]), correct_part, correct_got)
    low_solution = own_side(low_pair)
    root_out[:, 0, :] = low_solution
    share_pieces(CORRECT_SUM, CORRECT_SHARE, correct_part, correct_got, correct_share)
    share(LOW_ALL, low_solution, low_all)
    residual = whole_pieces(top_share) - shared_pieces(CORRECT_SHARE, correct_share)
    back = product_transposed(residual, root_stacked[top_inverse])
    share_quad(TOP_BACK_QUAD, back, top_back_quad)
    share_pair(LOW_ALL, low_all)
    top_solution = own_side(total_quad(TOP_BACK_QUAD, top_back_quad))
    share(TOP_ALL, top_solution, top_all)
    root_out[:, 1, :] = top_solution
    lifted = half_product(low_all, fc_stacked.at[0], core)
    pair_arrived(LOW_ALL, low_all)
    lifted = lifted + half_product(low_all, fc_stacked.at[0], other)

    lifted = lifted + gathered_product(TOP_ALL, top_all, fc_stacked.at[1])
    share(REMAINDER_ALL, front_forward - lifted, remainder_all)
    share(FRONT_ALL, gathered_product(REMAINDER_ALL, remainder_all, fi_stacked), front_all)
    share_pair(FRONT_ALL, front_all)
    pair_arrived(FRONT_ALL, front_all)
    for owner in range(devs):
        front_out[:, owner * front_part : (owner + 1) * front_part] = front_all[
            owner % 2, owner // 2
        ]

    solutions = [None] * blocks_here
    for k in reversed(range(blocks_here)):
        picked = jnp.zeros((columns, width), F32)
        for block in range(blocks_front):
            picked = picked + jnp.where(
                targets[k] == block, front_out[:, block * width : (block + 1) * width], 0.0
            )
        residual = solved[k] - product_transposed(picked, stack(leaf_front[k]))
        if k < blocks_here - 1:
            above = jnp.zeros((columns, width), F32)
            for upper in range(k + 1, blocks_here):
                above = above + jnp.where(parents[k] == upper, solutions[upper], 0.0)
            residual = residual - product_transposed(above, stack(leaf_link[k]))
        solutions[k] = jnp.where(k < live, product_transposed(residual, stack(leaf_inverse[k])), 0.0)
        leaf_out[:, k * width : (k + 1) * width] = solutions[k]

    for phase, buffer in (
        (FRONT_SUM, front_sum_part),
        (FRONT_SOLVE, front_solve_part),
        (RAISE_TOP, raise_top_part),
        (RAISE_LOW, raise_low_part),
        (LOW_ALL, low_all),
        (TOP_ALL, top_all),
        (REMAINDER_ALL, remainder_all),
        (FRONT_ALL, front_all),
    ):
        settle(send_sem.at[phase], buffer.at[0, pl.ds(1, chips - 1)])
        settle(pair_send_sem.at[phase], buffer.at[0])
    for phase, buffer in (
        (TOP_SUM, top_part),
        (TOP_SHARE, top_share),
        (LOW_SUM, low_part),
        (LOW_SHARE, low_share),
        (CORRECT_SUM, correct_part),
        (CORRECT_SHARE, correct_share),
    ):
        settle(send_sem.at[phase], buffer.at[pl.ds(1, chips - 1)])
    for phase, buffer in (
        (RAISE_TOP_QUAD, raise_top_quad),
        (RAISE_LOW_QUAD, raise_low_quad),
        (PUSH_QUAD, push_quad),
        (LOW_BACK_QUAD, low_back_quad),
        (TOP_BACK_QUAD, top_back_quad),
    ):
        settle(send_sem.at[phase], buffer.at[pl.ds(1, quads - 1)])
    settle(pair_send_sem.at[ROOT_SWAP], root_halves.at[:, 0])


def hand_on(*refs):
    semaphores = refs[-1]
    count = (len(refs) - 1) // 2
    copies = [
        pltpu.make_async_copy(refs[place], refs[count + place], semaphores.at[place])
        for place in range(count)
    ]
    for copy in copies:
        copy.start()
    for copy in copies:
        copy.wait()


def body(
    groups,
    devs,
    leaf_right,
    leaf_inverse,
    leaf_link,
    leaf_front,
    parents,
    front_rows,
    live_blocks,
    front_right,
    front_inverse,
    front_couple,
    root_right,
    root_inverse,
    root_couple,
):
    columns = leaf_right.shape[0]
    front_part = front_right.shape[1]
    level_part = root_right.shape[2]
    level_columns = root_inverse.shape[2]
    row_tiles = columns // ROW_TILE
    piece = level_columns // 2 * row_tiles // (devs // 2)
    loaded = (
        leaf_right,
        leaf_inverse,
        leaf_link,
        leaf_front,
        front_right,
        front_inverse,
        front_couple,
        root_inverse,
        root_couple,
    )
    rows, half = front_inverse.shape[0], front_inverse.shape[1] // 2
    level_half = front_couple.shape[1] // 4
    root_rows, root_half = root_inverse.shape[1], level_columns // 2
    halves = (
        (2, 2 * rows, half),
        (2, 2, 2 * rows, level_half),
        (3, 4 * root_rows, root_half),
    )
    chips = devs // 2
    front_full = pltpu.VMEM((2, chips, columns, front_part), F32)
    front_half = pltpu.VMEM((chips, columns, front_part), F32)
    level_full = pltpu.VMEM((2, chips, columns, level_part), F32)
    level_half_blocks = pltpu.VMEM((chips, columns, level_part), F32)
    pieces_half = pltpu.VMEM((chips, ROW_TILE, piece), F32)
    quad_blocks = pltpu.VMEM((2 * groups, columns, level_part), F32)
    quad_pairs = pltpu.VMEM((2 * groups, columns, 2 * level_part), F32)
    vmem = pl.BlockSpec(memory_space=pltpu.VMEM)
    smem = pl.BlockSpec(memory_space=pltpu.SMEM)
    anywhere = pl.BlockSpec(memory_space=pl.ANY)
    results = (
        jax.ShapeDtypeStruct(leaf_right.shape, F32),
        jax.ShapeDtypeStruct((columns, front_part * devs), F32),
        jax.ShapeDtypeStruct(root_right.shape, F32),
    )
    solutions = pl.pallas_call(
        functools.partial(kernel, groups, devs),
        out_shape=results,
        in_specs=[smem] * 3 + [vmem] + [anywhere] * len(loaded),
        out_specs=(vmem, vmem, vmem),
        scratch_shapes=[pltpu.VMEM(array.shape, F32) for array in loaded[:-2]]
        + [pltpu.VMEM((3, 2, root_rows, root_half), F32)]
        + [pltpu.VMEM(shape, BF16) for shape in halves]
        + [pltpu.VMEM((leaf_inverse.shape[0], columns, leaf_inverse.shape[1]), F32)]
        + [front_full] * 2
        + [front_half] * 4
        + [level_full] * 2
        + [level_half_blocks] * 4
        + [pieces_half] * 9
        + [quad_blocks] * 2
        + [quad_pairs] * 3
        + [level_full] * 2
        + [front_full] * 2
        + [
            pltpu.SemaphoreType.DMA((len(loaded) + 1,)),
        ]
        + [pltpu.SemaphoreType.DMA((PHASES,))] * 4,
        compiler_params=pltpu.CompilerParams(
            collective_id=0, has_side_effects=True, vmem_limit_bytes=62 * 1024 * 1024
        ),
        name="block_solves",
    )(parents, front_rows, live_blocks, root_right, *loaded)
    return pl.pallas_call(
        hand_on,
        out_shape=results,
        in_specs=[anywhere] * len(results),
        out_specs=(anywhere,) * len(results),
        scratch_shapes=[pltpu.SemaphoreType.DMA((len(results),))],
        compiler_params=pltpu.CompilerParams(vmem_limit_bytes=62 * 1024 * 1024),
        name="hand_on",
    )(*solutions)


def solution(mesh):
    in_specs = (
        P(None, ("grp", "dev")),
        P(("grp", "dev"), None, None),
        P(("grp", "dev"), None, None),
        P(("grp", "dev"), None, None),
        P(("grp", "dev")),
        P(("grp", "dev")),
        P(("grp", "dev")),
        P(None, ("grp", "dev")),
        P(("grp", "dev"), None),
        P(("grp", "dev"), None),
        P(None, None, "dev"),
        P(None, "dev", "grp"),
        P(None, "dev", "grp"),
    )
    out_specs = (P(None, ("grp", "dev")), P(None, "grp"), P(None, None, "dev"))
    return jax.shard_map(
        functools.partial(body, mesh.shape["grp"], mesh.shape["dev"]),
        mesh=mesh,
        in_specs=in_specs,
        out_specs=out_specs,
        check_vma=False,
    )
```

```python
import functools

import jax
import jax.numpy as jnp
from jax import lax
from jax.experimental import pallas as pl
from jax.experimental.pallas import tpu as pltpu
from jax.sharding import PartitionSpec as P

MESH = pl.DeviceIdType.MESH
ROW_TILE = 8
STREAMS = 2
F32 = jnp.float32
BF16 = jnp.bfloat16

(
    FRONT_SUM,
    FRONT_SOLVE,
    RAISE_TOP,
    RAISE_LOW,
    RAISE_TOP_QUAD,
    RAISE_LOW_QUAD,
    TOP_SUM,
    TOP_SHARE,
    PUSH_QUAD,
    LOW_SUM,
    LOW_SHARE,
    LOW_BACK_QUAD,
    CORRECT_SUM,
    CORRECT_SHARE,
    LOW_ALL,
    TOP_BACK_QUAD,
    TOP_ALL,
    REMAINDER_ALL,
    FRONT_ALL,
    ROOT_SWAP,
    PHASES,
) = range(21)


def split(values):
    high = values.astype(BF16)
    return high, (values - high.astype(F32)).astype(BF16)


def product(left, stacked):
    rows = left.shape[0]
    high, low = split(left)
    both = jnp.concatenate(
        [jnp.concatenate([high, high], 1), jnp.concatenate([low, low], 1)], 0
    )
    result = jnp.dot(both, stacked, preferred_element_type=F32)
    return result[:rows] + result[rows:]


def product_transposed(left, stacked):
    rows, depth = left.shape[0], stacked.shape[0] // 2
    result = lax.dot_general(
        jnp.concatenate(split(left), 0),
        stacked,
        (((1,), (1,)), ((), ())),
        preferred_element_type=F32,
    )
    result = result[:rows] + result[rows:]
    return result[:, :depth] + result[:, depth:]


def stack(values):
    return jnp.concatenate(split(values), 0)


def kernel(
    groups,
    devs,
    parents,
    targets,
    live_blocks,
    root_right,
    leaf_right_hbm,
    leaf_inverse_hbm,
    leaf_link_hbm,
    leaf_front_hbm,
    front_right_hbm,
    front_inverse_hbm,
    front_couple_hbm,
    root_inverse_hbm,
    root_couple_hbm,
    leaf_out,
    front_out,
    root_out,
    leaf_right,
    leaf_inverse,
    leaf_link,
    leaf_front,
    front_right,
    front_inverse,
    front_couple,
    root_halves,
    fi_stacked,
    fc_stacked,
    root_stacked,
    *rest,
):
    *buffers, load_sem, send_sem, recv_sem, pair_send_sem, pair_recv_sem = rest
    group = lax.axis_index("grp")
    me = lax.axis_index("dev")
    chips = devs // 2
    chip = me // 2
    core = lax.rem(me, 2)
    other = 1 - core
    sibling = (group, chip * 2 + other)
    quad = group * 2 + core
    columns = leaf_right.shape[0] // STREAMS
    blocks_here, width = leaf_inverse.shape[0], leaf_inverse.shape[1]
    blocks_front = front_inverse.shape[1] // width
    front_part = front_right.shape[1]
    level_rows = front_couple.shape[1] // 2
    row_tiles = columns // ROW_TILE
    half = root_halves.shape[3]
    quads = 2 * groups
    piece = half * row_tiles // chips
    low_inverse, top_inverse, couple = range(3)

    def chip_peer(step):
        return (group, lax.rem(chip + step, chips) * 2 + core)

    def quad_peer(step):
        peer = lax.rem(quad + step, quads)
        return (peer // 2, chip * 2 + lax.rem(peer, 2))

    def half_of(matrix, side):
        columns_of = pl.ds(pl.multiple_of(side * half, half), half)
        if matrix == couple:
            return root_couple_hbm.at[0, :, columns_of]
        return root_inverse_hbm.at[matrix, :, columns_of]

    loads = [
        pltpu.make_async_copy(source, target, load_sem.at[place])
        for place, (source, target) in enumerate(
            (
                (leaf_right_hbm, leaf_right),
                (leaf_inverse_hbm, leaf_inverse),
                (leaf_link_hbm, leaf_link),
                (leaf_front_hbm, leaf_front),
                (front_right_hbm, front_right),
                (front_inverse_hbm, front_inverse),
                (front_couple_hbm, front_couple),
                (half_of(low_inverse, core), root_halves.at[low_inverse, core]),
                (half_of(top_inverse, core), root_halves.at[top_inverse, core]),
                (half_of(couple, core), root_halves.at[couple, core]),
            )
        )
    ]
    for load in loads:
        load.start()

    barrier = pltpu.get_barrier_semaphore()

    def greet(device):
        pl.semaphore_signal(barrier, inc=1, device_id=device, device_id_type=MESH)

    for step in range(1, chips):
        greet(chip_peer(step))
    for step in range(1, quads):
        greet(quad_peer(step))

    def solve(stream):
        own_rows = slice(stream * columns, (stream + 1) * columns)
        (
            solved,
            front_sum_part,
            front_solve_part,
            front_sum_pair,
            front_sum_got,
            front_solve_pair,
            front_solve_got,
            raise_top_part,
            raise_low_part,
            raise_top_pair,
            raise_top_got,
            raise_low_pair,
            raise_low_got,
            top_part,
            low_part,
            correct_part,
            top_got,
            low_got,
            correct_got,
            top_share,
            low_share,
            correct_share,
            raise_top_quad,
            raise_low_quad,
            push_quad,
            low_back_quad,
            top_back_quad,
            low_all,
            top_all,
            remainder_all,
            front_all,
        ) = [buffer.at[stream] for buffer in buffers]

        def send(source, target, device, phase):
            pltpu.make_async_remote_copy(
                src_ref=source,
                dst_ref=target,
                send_sem=send_sem.at[stream, phase],
                recv_sem=recv_sem.at[stream, phase],
                device_id=device,
                device_id_type=MESH,
            ).start()

        def send_pair(source, target, phase):
            pltpu.make_async_remote_copy(
                src_ref=source,
                dst_ref=target,
                send_sem=pair_send_sem.at[stream, phase],
                recv_sem=pair_recv_sem.at[stream, phase],
                device_id=sibling,
                device_id_type=MESH,
            ).start()

        def settle(semaphore, some):
            pltpu.make_async_copy(some, some, semaphore).wait()

        def pair_sum(phase, part, pair, fill):
            fill(other, part.at[other])
            send_pair(part.at[other], pair, phase)
            fill(core, part.at[core])

        def chip_send(phase, part, got):
            for step in range(1, chips):
                peer = lax.rem(chip + step, chips)
                send(part.at[core, peer], got.at[step], chip_peer(step), phase)

        def pair_done(phase, part, pair):
            settle(pair_recv_sem.at[stream, phase], pair)
            for place in range(chips):
                part[core, place] = part[core, place] + pair[place]

        def total(phase, part, got):
            result = part[core, chip]
            settle(recv_sem.at[stream, phase], got.at[pl.ds(1, chips - 1)])
            for place in range(1, chips):
                result = result + got[place]
            return result

        def share(phase, values, buffer):
            buffer[core, chip] = values
            for step in range(1, chips):
                send(buffer.at[core, chip], buffer.at[core, chip], chip_peer(step), phase)

        def share_pair(phase, buffer):
            settle(recv_sem.at[stream, phase], buffer.at[0, pl.ds(1, chips - 1)])
            send_pair(buffer.at[core], buffer.at[core], phase)

        def pair_arrived(phase, buffer):
            settle(pair_recv_sem.at[stream, phase], buffer.at[0])

        def share_quad(phase, values, buffer):
            buffer[quad] = values
            for step in range(1, quads):
                send(buffer.at[quad], buffer.at[quad], quad_peer(step), phase)

        def quad_wait(phase, buffer):
            settle(recv_sem.at[stream, phase], buffer.at[pl.ds(1, quads - 1)])

        def total_quad(phase, buffer):
            quad_wait(phase, buffer)
            result = buffer[0]
            for place in range(1, quads):
                result = result + buffer[place]
            return result

        def pair_quad(phase, buffer):
            quad_wait(phase, buffer)
            sides = []
            for side in range(2):
                result = buffer[side]
                for place in range(1, groups):
                    result = result + buffer[2 * place + side]
                sides.append(result)
            return jnp.concatenate(sides, 1)

        def own_side(values):
            part = values.shape[1] // 2
            return jnp.where(core == 0, values[:, :part], values[:, part:])

        def whole(buffer, side):
            return jnp.concatenate([buffer[side, place] for place in range(chips)], 1)

        def split_rows(source, stacked, span, column=0):
            step_rows = 2 * ROW_TILE
            count = source.shape[0]

            def one(step, carry):
                at_rows = pl.multiple_of(step * step_rows, step_rows)
                rows = pl.ds(at_rows, step_rows)
                rows_low = pl.ds(pl.multiple_of(at_rows + count, step_rows), step_rows)
                for at in range(0, 2 * stacked.shape[2], span):
                    parity, place = (at // span) % 2, at // span // 2 * span
                    upper, lower = split(source[rows, column + at : column + at + span])
                    stacked[parity, rows, place : place + span] = upper
                    stacked[parity, rows_low, place : place + span] = lower
                return carry

            lax.fori_loop(0, count // step_rows, one, 0)

        def split_root(matrix):
            step_rows = 2 * ROW_TILE
            count = root_halves.shape[2]

            def one(step, carry):
                at_rows = pl.multiple_of(step * step_rows, step_rows)
                for side in range(2):
                    upper, lower = split(root_halves[matrix, side, pl.ds(at_rows, step_rows), :])
                    for start, values in ((side, upper), (side + 2, lower)):
                        rows = pl.multiple_of(at_rows + start * count, step_rows)
                        root_stacked[matrix, pl.ds(rows, step_rows), :] = values
                return carry

            lax.fori_loop(0, count // step_rows, one, 0)

        def fill_blocks(left, stacked):
            def fill(side, part):
                count, span = part.shape[0], part.shape[2]
                chunk = min(count * span, 512)
                for at in range(0, count * span, chunk):
                    here = product(left, stacked[side, :, at : at + chunk])
                    for block in range(chunk // span):
                        part[at // span + block] = here[:, block * span : (block + 1) * span]

            return fill

        def send_pieces(phase, values, part, got):
            for across in range(chips // row_tiles):
                for down in range(row_tiles):
                    part[across * row_tiles + down] = values[
                        down * ROW_TILE : (down + 1) * ROW_TILE,
                        across * piece : (across + 1) * piece,
                    ]
            for step in range(1, chips):
                send(part.at[lax.rem(chip + step, chips)], got.at[step], chip_peer(step), phase)

        def share_pieces(phase, share_phase, part, got, buffer):
            settle(recv_sem.at[stream, phase], got.at[pl.ds(1, chips - 1)])
            result = part[chip]
            for place in range(1, chips):
                result = result + got[place]
            buffer[chip] = result
            for step in range(1, chips):
                send(buffer.at[chip], buffer.at[chip], chip_peer(step), share_phase)

        def whole_pieces(buffer):
            return jnp.concatenate(
                [
                    jnp.concatenate([buffer[across * row_tiles + down] for down in range(row_tiles)], 0)
                    for across in range(chips // row_tiles)
                ],
                1,
            )

        def shared_pieces(phase, buffer):
            settle(recv_sem.at[stream, phase], buffer.at[pl.ds(1, chips - 1)])
            return whole_pieces(buffer)

        def half_product(buffer, stacked, side):
            return product_transposed(whole(buffer, side), stacked[side])

        def gathered_product(phase, buffer, stacked):
            yield
            share_pair(phase, buffer)
            result = half_product(buffer, stacked, core)
            yield
            pair_arrived(phase, buffer)
            return result + half_product(buffer, stacked, other)

        live = live_blocks[0]
        if stream == 0:
            for place in range(4):
                loads[place].wait()
        updates = []
        contributions = []
        for k in range(blocks_here):
            residual = leaf_right[own_rows, k * width : (k + 1) * width]
            for child in range(k):
                residual = residual - jnp.where(parents[child] == k, updates[child], 0.0)
            block = jnp.where(k < live, product(residual, stack(leaf_inverse[k])), 0.0)
            solved[k] = block
            if k < blocks_here - 1:
                updates.append(product(block, stack(leaf_link[k])))
            contributions.append(product(block, stack(leaf_front[k])))
        spans = width // front_part
        for block in range(blocks_front):
            placed = jnp.zeros((columns, width), F32)
            for k in range(blocks_here):
                placed = placed + jnp.where(targets[k] == block, contributions[k], 0.0)
            for within in range(spans):
                owner = block * spans + within
                front_sum_part[owner % 2, owner // 2] = placed[
                    :, within * front_part : (within + 1) * front_part
                ]

        if stream == 0:
            pl.semaphore_wait(barrier, chips - 1 + quads - 1)
        send_pair(front_sum_part.at[other], front_sum_pair, FRONT_SUM)
        yield
        if stream == 0:
            loads[4].wait()
            loads[5].wait()
        pair_done(FRONT_SUM, front_sum_part, front_sum_pair)
        chip_send(FRONT_SUM, front_sum_part, front_sum_got)

        if stream == 0:
            split_rows(front_inverse, fi_stacked, front_part)
            for matrix in range(3):
                send_pair(half_of(matrix, other), root_halves.at[matrix, core], ROOT_SWAP)
        yield
        residual = front_right[own_rows, :] - total(FRONT_SUM, front_sum_part, front_sum_got)
        pair_sum(FRONT_SOLVE, front_solve_part, front_solve_pair, fill_blocks(residual, fi_stacked))
        yield
        pair_done(FRONT_SOLVE, front_solve_part, front_solve_pair)
        chip_send(FRONT_SOLVE, front_solve_part, front_solve_got)
        if stream == 0:
            loads[6].wait()
            level_part = level_rows // devs
            for level in range(2):
                split_rows(front_couple, fc_stacked.at[level], level_part, level * level_rows)
        yield
        front_forward = total(FRONT_SOLVE, front_solve_part, front_solve_got)

        pair_sum(
            RAISE_TOP, raise_top_part, raise_top_pair, fill_blocks(front_forward, fc_stacked.at[1])
        )
        yield
        pair_done(RAISE_TOP, raise_top_part, raise_top_pair)
        chip_send(RAISE_TOP, raise_top_part, raise_top_got)
        pair_sum(
            RAISE_LOW, raise_low_part, raise_low_pair, fill_blocks(front_forward, fc_stacked.at[0])
        )
        if stream == 0:
            for place in (7, 8, 9):
                loads[place].wait()
            settle(pair_recv_sem.at[stream, ROOT_SWAP], root_halves.at[:, 0])
            for matrix in range(3):
                split_root(matrix)
        yield
        pair_done(RAISE_LOW, raise_low_part, raise_low_pair)

        def less_right(level, values):
            return values - jnp.where(group == 0, root_right[own_rows, level, :], 0.0)

        yield
        raised_top = total(RAISE_TOP, raise_top_part, raise_top_got)
        share_quad(RAISE_TOP_QUAD, less_right(1, raised_top), raise_top_quad)
        chip_send(RAISE_LOW, raise_low_part, raise_low_got)

        yield
        residual = -pair_quad(RAISE_TOP_QUAD, raise_top_quad)
        send_pieces(TOP_SUM, product(residual, root_stacked[top_inverse]), top_part, top_got)
        raised_low = total(RAISE_LOW, raise_low_part, raise_low_got)
        share_quad(RAISE_LOW_QUAD, less_right(0, raised_low), raise_low_quad)
        yield
        share_pieces(TOP_SUM, TOP_SHARE, top_part, top_got, top_share)
        low_right = -pair_quad(RAISE_LOW_QUAD, raise_low_quad)

        yield
        top_forward = shared_pieces(TOP_SHARE, top_share)
        share_quad(PUSH_QUAD, product_transposed(top_forward, root_stacked[couple]), push_quad)
        yield
        residual = low_right - total_quad(PUSH_QUAD, push_quad)
        send_pieces(LOW_SUM, product(residual, root_stacked[low_inverse]), low_part, low_got)
        yield
        share_pieces(LOW_SUM, LOW_SHARE, low_part, low_got, low_share)

        yield
        low_forward = shared_pieces(LOW_SHARE, low_share)
        back = product_transposed(low_forward, root_stacked[low_inverse])
        share_quad(LOW_BACK_QUAD, back, low_back_quad)
        yield
        low_pair = total_quad(LOW_BACK_QUAD, low_back_quad)
        send_pieces(CORRECT_SUM, product(low_pair, root_stacked[couple]), correct_part, correct_got)
        low_solution = own_side(low_pair)
        root_out[own_rows, 0, :] = low_solution
        yield
        share_pieces(CORRECT_SUM, CORRECT_SHARE, correct_part, correct_got, correct_share)
        share(LOW_ALL, low_solution, low_all)
        yield
        residual = whole_pieces(top_share) - shared_pieces(CORRECT_SHARE, correct_share)
        back = product_transposed(residual, root_stacked[top_inverse])
        share_quad(TOP_BACK_QUAD, back, top_back_quad)
        share_pair(LOW_ALL, low_all)
        yield
        top_solution = own_side(total_quad(TOP_BACK_QUAD, top_back_quad))
        share(TOP_ALL, top_solution, top_all)
        root_out[own_rows, 1, :] = top_solution
        lifted = half_product(low_all, fc_stacked.at[0], core)
        pair_arrived(LOW_ALL, low_all)
        lifted = lifted + half_product(low_all, fc_stacked.at[0], other)

        lifted = lifted + (yield from gathered_product(TOP_ALL, top_all, fc_stacked.at[1]))
        share(REMAINDER_ALL, front_forward - lifted, remainder_all)
        front_values = yield from gathered_product(REMAINDER_ALL, remainder_all, fi_stacked)
        share(FRONT_ALL, front_values, front_all)
        yield
        share_pair(FRONT_ALL, front_all)
        yield
        pair_arrived(FRONT_ALL, front_all)
        for owner in range(devs):
            front_out[own_rows, owner * front_part : (owner + 1) * front_part] = front_all[
                owner % 2, owner // 2
            ]

        solutions = [None] * blocks_here
        for k in reversed(range(blocks_here)):
            picked = jnp.zeros((columns, width), F32)
            for block in range(blocks_front):
                picked = picked + jnp.where(
                    targets[k] == block, front_out[own_rows, block * width : (block + 1) * width], 0.0
                )
            residual = solved[k] - product_transposed(picked, stack(leaf_front[k]))
            if k < blocks_here - 1:
                above = jnp.zeros((columns, width), F32)
                for upper in range(k + 1, blocks_here):
                    above = above + jnp.where(parents[k] == upper, solutions[upper], 0.0)
                residual = residual - product_transposed(above, stack(leaf_link[k]))
            solutions[k] = jnp.where(k < live, product_transposed(residual, stack(leaf_inverse[k])), 0.0)
            leaf_out[own_rows, k * width : (k + 1) * width] = solutions[k]

        yield
        for phase, buffer in (
            (FRONT_SUM, front_sum_part),
            (FRONT_SOLVE, front_solve_part),
            (RAISE_TOP, raise_top_part),
            (RAISE_LOW, raise_low_part),
            (LOW_ALL, low_all),
            (TOP_ALL, top_all),
            (REMAINDER_ALL, remainder_all),
            (FRONT_ALL, front_all),
        ):
            settle(send_sem.at[stream, phase], buffer.at[0, pl.ds(1, chips - 1)])
            settle(pair_send_sem.at[stream, phase], buffer.at[0])
        for phase, buffer in (
            (TOP_SUM, top_part),
            (TOP_SHARE, top_share),
            (LOW_SUM, low_part),
            (LOW_SHARE, low_share),
            (CORRECT_SUM, correct_part),
            (CORRECT_SHARE, correct_share),
        ):
            settle(send_sem.at[stream, phase], buffer.at[pl.ds(1, chips - 1)])
        for phase, buffer in (
            (RAISE_TOP_QUAD, raise_top_quad),
            (RAISE_LOW_QUAD, raise_low_quad),
            (PUSH_QUAD, push_quad),
            (LOW_BACK_QUAD, low_back_quad),
            (TOP_BACK_QUAD, top_back_quad),
        ):
            settle(send_sem.at[stream, phase], buffer.at[pl.ds(1, quads - 1)])
        if stream == 0:
            settle(pair_send_sem.at[stream, ROOT_SWAP], root_halves.at[:, 0])

    waiting = [solve(stream) for stream in range(STREAMS)]
    while waiting:
        waiting = [steps for steps in waiting if next(steps, True) is None]


def body(
    groups,
    devs,
    leaf_right,
    leaf_inverse,
    leaf_link,
    leaf_front,
    parents,
    front_rows,
    live_blocks,
    front_right,
    front_inverse,
    front_couple,
    root_right,
    root_inverse,
    root_couple,
):
    columns = leaf_right.shape[0]
    front_part = front_right.shape[1]
    level_part = root_right.shape[2]
    level_columns = root_inverse.shape[2]
    row_tiles = columns // STREAMS // ROW_TILE
    piece = level_columns // 2 * row_tiles // (devs // 2)
    own = columns // STREAMS
    loaded = (
        leaf_right,
        leaf_inverse,
        leaf_link,
        leaf_front,
        front_right,
        front_inverse,
        front_couple,
        root_inverse,
        root_couple,
    )
    rows, half = front_inverse.shape[0], front_inverse.shape[1] // 2
    level_half = front_couple.shape[1] // 4
    root_rows, root_half = root_inverse.shape[1], level_columns // 2
    halves = (
        (2, 2 * rows, half),
        (2, 2, 2 * rows, level_half),
        (3, 4 * root_rows, root_half),
    )
    chips = devs // 2
    front_full = pltpu.VMEM((STREAMS, 2, chips, own, front_part), F32)
    front_half = pltpu.VMEM((STREAMS, chips, own, front_part), F32)
    level_full = pltpu.VMEM((STREAMS, 2, chips, own, level_part), F32)
    level_half_blocks = pltpu.VMEM((STREAMS, chips, own, level_part), F32)
    pieces_half = pltpu.VMEM((STREAMS, chips, ROW_TILE, piece), F32)
    quad_blocks = pltpu.VMEM((STREAMS, 2 * groups, own, level_part), F32)
    quad_pairs = pltpu.VMEM((STREAMS, 2 * groups, own, 2 * level_part), F32)
    vmem = pl.BlockSpec(memory_space=pltpu.VMEM)
    smem = pl.BlockSpec(memory_space=pltpu.SMEM)
    anywhere = pl.BlockSpec(memory_space=pltpu.HBM)
    results = (
        jax.ShapeDtypeStruct(leaf_right.shape, F32),
        jax.ShapeDtypeStruct((columns, front_part * devs), F32),
        jax.ShapeDtypeStruct(root_right.shape, F32),
    )
    return pl.pallas_call(
        functools.partial(kernel, groups, devs),
        out_shape=results,
        in_specs=[smem] * 3 + [vmem] + [anywhere] * len(loaded),
        out_specs=(vmem, vmem, vmem),
        scratch_shapes=[pltpu.VMEM(array.shape, F32) for array in loaded[:-2]]
        + [pltpu.VMEM((3, 2, root_rows, root_half), F32)]
        + [pltpu.VMEM(shape, BF16) for shape in halves]
        + [pltpu.VMEM((STREAMS, leaf_inverse.shape[0], own, leaf_inverse.shape[1]), F32)]
        + [front_full] * 2
        + [front_half] * 4
        + [level_full] * 2
        + [level_half_blocks] * 4
        + [pieces_half] * 9
        + [quad_blocks] * 2
        + [quad_pairs] * 3
        + [level_full] * 2
        + [front_full] * 2
        + [
            pltpu.SemaphoreType.DMA((len(loaded) + 1,)),
        ]
        + [pltpu.SemaphoreType.DMA((STREAMS, PHASES))] * 4,
        compiler_params=pltpu.CompilerParams(
            collective_id=0, has_side_effects=True, vmem_limit_bytes=60 * 1024 * 1024
        ),
        name="block_solves",
    )(parents, front_rows, live_blocks, root_right, *loaded)


def solution(mesh):
    in_specs = (
        P(None, ("grp", "dev")),
        P(("grp", "dev"), None, None),
        P(("grp", "dev"), None, None),
        P(("grp", "dev"), None, None),
        P(("grp", "dev")),
        P(("grp", "dev")),
        P(("grp", "dev")),
        P(None, ("grp", "dev")),
        P(("grp", "dev"), None),
        P(("grp", "dev"), None),
        P(None, None, "dev"),
        P(None, "dev", "grp"),
        P(None, "dev", "grp"),
    )
    out_specs = (P(None, ("grp", "dev")), P(None, "grp"), P(None, None, "dev"))
    return jax.shard_map(
        functools.partial(body, mesh.shape["grp"], mesh.shape["dev"]),
        mesh=mesh,
        in_specs=in_specs,
        out_specs=out_specs,
        check_vma=False,
    )
```

```python
import functools

import jax
import jax.numpy as jnp
from jax import lax
from jax.experimental import pallas as pl
from jax.experimental.pallas import tpu as pltpu
from jax.sharding import PartitionSpec as P

MESH = pl.DeviceIdType.MESH
ROW_TILE = 8
STREAMS = 2
F32 = jnp.float32
BF16 = jnp.bfloat16

(
    FRONT_SUM,
    FRONT_SOLVE,
    RAISE_TOP,
    RAISE_LOW,
    RAISE_TOP_QUAD,
    RAISE_LOW_QUAD,
    TOP_SUM,
    TOP_SHARE,
    PUSH_QUAD,
    LOW_SUM,
    LOW_SHARE,
    LOW_BACK_QUAD,
    CORRECT_SUM,
    CORRECT_SHARE,
    LOW_ALL,
    TOP_BACK_QUAD,
    TOP_ALL,
    REMAINDER_ALL,
    FRONT_ALL,
    ROOT_SWAP,
    PHASES,
) = range(21)


def split(values):
    high = values.astype(BF16)
    return high, (values - high.astype(F32)).astype(BF16)


def product(left, stacked):
    rows = left.shape[0]
    high, low = split(left)
    both = jnp.concatenate(
        [jnp.concatenate([high, high], 1), jnp.concatenate([low, low], 1)], 0
    )
    result = jnp.dot(both, stacked, preferred_element_type=F32)
    return result[:rows] + result[rows:]


def product_transposed(left, stacked):
    rows, depth = left.shape[0], stacked.shape[0] // 2
    result = lax.dot_general(
        jnp.concatenate(split(left), 0),
        stacked,
        (((1,), (1,)), ((), ())),
        preferred_element_type=F32,
    )
    result = result[:rows] + result[rows:]
    return result[:, :depth] + result[:, depth:]


def product_turned(left, turned):
    rows, width = left.shape[0], turned.shape[1] // 2
    result = jnp.dot(jnp.concatenate(split(left), 0), turned, preferred_element_type=F32)
    result = result[:rows] + result[rows:]
    return result[:, :width] + result[:, width:]


def stack(values):
    return jnp.concatenate(split(values), 0)


def kernel(
    groups,
    devs,
    parents,
    targets,
    live_blocks,
    root_right,
    leaf_right_hbm,
    leaf_inverse_hbm,
    leaf_link_hbm,
    leaf_front_hbm,
    front_right_hbm,
    front_inverse_hbm,
    front_couple_hbm,
    root_inverse_hbm,
    root_couple_hbm,
    leaf_out,
    front_out,
    root_out,
    leaf_right,
    leaf_inverse,
    leaf_link,
    leaf_front,
    front_right,
    front_inverse,
    front_couple,
    root_halves,
    fi_stacked,
    fc_stacked,
    root_stacked,
    fi_turned,
    fc_turned,
    root_turned,
    *rest,
):
    *buffers, load_sem, send_sem, recv_sem, pair_send_sem, pair_recv_sem = rest
    group = lax.axis_index("grp")
    me = lax.axis_index("dev")
    chips = devs // 2
    chip = me // 2
    core = lax.rem(me, 2)
    other = 1 - core
    sibling = (group, chip * 2 + other)
    quad = group * 2 + core
    columns = leaf_right.shape[0] // STREAMS
    blocks_here, width = leaf_inverse.shape[0], leaf_inverse.shape[1]
    blocks_front = front_inverse.shape[1] // width
    front_part = front_right.shape[1]
    level_rows = front_couple.shape[1] // 2
    row_tiles = columns // ROW_TILE
    half = root_halves.shape[3]
    quads = 2 * groups
    piece = half * row_tiles // chips
    low_inverse, top_inverse, couple = range(3)

    def chip_peer(step):
        return (group, lax.rem(chip + step, chips) * 2 + core)

    def quad_peer(step):
        peer = lax.rem(quad + step, quads)
        return (peer // 2, chip * 2 + lax.rem(peer, 2))

    def half_of(matrix, side):
        columns_of = pl.ds(pl.multiple_of(side * half, half), half)
        if matrix == couple:
            return root_couple_hbm.at[0, :, columns_of]
        return root_inverse_hbm.at[matrix, :, columns_of]

    loads = [
        pltpu.make_async_copy(source, target, load_sem.at[place])
        for place, (source, target) in enumerate(
            (
                (leaf_right_hbm, leaf_right),
                (leaf_inverse_hbm, leaf_inverse),
                (leaf_link_hbm, leaf_link),
                (leaf_front_hbm, leaf_front),
                (front_right_hbm, front_right),
                (front_inverse_hbm, front_inverse),
                (front_couple_hbm, front_couple),
                (half_of(low_inverse, core), root_halves.at[low_inverse, core]),
                (half_of(top_inverse, core), root_halves.at[top_inverse, core]),
                (half_of(couple, core), root_halves.at[couple, core]),
            )
        )
    ]
    for load in loads:
        load.start()

    barrier = pltpu.get_barrier_semaphore()

    def greet(device):
        pl.semaphore_signal(barrier, inc=1, device_id=device, device_id_type=MESH)

    for step in range(1, chips):
        greet(chip_peer(step))
    for step in range(1, quads):
        greet(quad_peer(step))

    def solve(stream):
        own_rows = slice(stream * columns, (stream + 1) * columns)
        (
            solved,
            front_sum_part,
            front_solve_part,
            front_sum_pair,
            front_sum_got,
            front_solve_pair,
            front_solve_got,
            raise_top_part,
            raise_low_part,
            raise_top_pair,
            raise_top_got,
            raise_low_pair,
            raise_low_got,
            top_part,
            low_part,
            correct_part,
            top_got,
            low_got,
            correct_got,
            top_share,
            low_share,
            correct_share,
            raise_top_quad,
            raise_low_quad,
            push_quad,
            low_back_quad,
            top_back_quad,
            low_all,
            top_all,
            remainder_all,
            front_all,
        ) = [buffer.at[stream] for buffer in buffers]

        def send(source, target, device, phase):
            pltpu.make_async_remote_copy(
                src_ref=source,
                dst_ref=target,
                send_sem=send_sem.at[stream, phase],
                recv_sem=recv_sem.at[stream, phase],
                device_id=device,
                device_id_type=MESH,
            ).start()

        def send_pair(source, target, phase):
            pltpu.make_async_remote_copy(
                src_ref=source,
                dst_ref=target,
                send_sem=pair_send_sem.at[stream, phase],
                recv_sem=pair_recv_sem.at[stream, phase],
                device_id=sibling,
                device_id_type=MESH,
            ).start()

        def settle(semaphore, some):
            pltpu.make_async_copy(some, some, semaphore).wait()

        def pair_sum(phase, part, pair, fill):
            fill(other, part.at[other])
            send_pair(part.at[other], pair, phase)
            fill(core, part.at[core])

        def chip_send(phase, part, got):
            for step in range(1, chips):
                peer = lax.rem(chip + step, chips)
                send(part.at[core, peer], got.at[step], chip_peer(step), phase)

        def pair_done(phase, part, pair):
            settle(pair_recv_sem.at[stream, phase], pair)
            for place in range(chips):
                part[core, place] = part[core, place] + pair[place]

        def total(phase, part, got):
            result = part[core, chip]
            settle(recv_sem.at[stream, phase], got.at[pl.ds(1, chips - 1)])
            for place in range(1, chips):
                result = result + got[place]
            return result

        def share(phase, values, buffer):
            buffer[core, chip] = values
            for step in range(1, chips):
                send(buffer.at[core, chip], buffer.at[core, chip], chip_peer(step), phase)

        def share_pair(phase, buffer):
            settle(recv_sem.at[stream, phase], buffer.at[0, pl.ds(1, chips - 1)])
            send_pair(buffer.at[core], buffer.at[core], phase)

        def pair_arrived(phase, buffer):
            settle(pair_recv_sem.at[stream, phase], buffer.at[0])

        def share_quad(phase, values, buffer):
            buffer[quad] = values
            for step in range(1, quads):
                send(buffer.at[quad], buffer.at[quad], quad_peer(step), phase)

        def quad_wait(phase, buffer):
            settle(recv_sem.at[stream, phase], buffer.at[pl.ds(1, quads - 1)])

        def total_quad(phase, buffer):
            quad_wait(phase, buffer)
            result = buffer[0]
            for place in range(1, quads):
                result = result + buffer[place]
            return result

        def pair_quad(phase, buffer):
            quad_wait(phase, buffer)
            sides = []
            for side in range(2):
                result = buffer[side]
                for place in range(1, groups):
                    result = result + buffer[2 * place + side]
                sides.append(result)
            return jnp.concatenate(sides, 1)

        def own_side(values):
            part = values.shape[1] // 2
            return jnp.where(core == 0, values[:, :part], values[:, part:])

        def whole(buffer, side):
            return jnp.concatenate([buffer[side, place] for place in range(chips)], 1)

        def split_rows(source, stacked, span, column=0):
            step_rows = 2 * ROW_TILE
            count = source.shape[0]

            def one(step, carry):
                at_rows = pl.multiple_of(step * step_rows, step_rows)
                rows = pl.ds(at_rows, step_rows)
                rows_low = pl.ds(pl.multiple_of(at_rows + count, step_rows), step_rows)
                for at in range(0, 2 * stacked.shape[2], span):
                    parity, place = (at // span) % 2, at // span // 2 * span
                    upper, lower = split(source[rows, column + at : column + at + span])
                    stacked[parity, rows, place : place + span] = upper
                    stacked[parity, rows_low, place : place + span] = lower
                return carry

            lax.fori_loop(0, count // step_rows, one, 0)

        def split_root(matrix):
            step_rows = 2 * ROW_TILE
            count = root_halves.shape[2]

            def one(step, carry):
                at_rows = pl.multiple_of(step * step_rows, step_rows)
                for side in range(2):
                    upper, lower = split(root_halves[matrix, side, pl.ds(at_rows, step_rows), :])
                    for start, values in ((side, upper), (side + 2, lower)):
                        rows = pl.multiple_of(at_rows + start * count, step_rows)
                        root_stacked[matrix, pl.ds(rows, step_rows), :] = values
                return carry

            lax.fori_loop(0, count // step_rows, one, 0)

        def turn(source, target):
            step = min(source.shape[1], 256)
            for at in range(0, source.shape[1], step):
                here = source[:, at : at + step].astype(F32)
                target[at : at + step, :] = here.T.astype(BF16)

        def fill_blocks(left, stacked):
            def fill(side, part):
                count, span = part.shape[0], part.shape[2]
                chunk = min(count * span, 512)
                for at in range(0, count * span, chunk):
                    here = product(left, stacked[side, :, at : at + chunk])
                    for block in range(chunk // span):
                        part[at // span + block] = here[:, block * span : (block + 1) * span]

            return fill

        def send_pieces(phase, values, part, got):
            for across in range(chips // row_tiles):
                for down in range(row_tiles):
                    part[across * row_tiles + down] = values[
                        down * ROW_TILE : (down + 1) * ROW_TILE,
                        across * piece : (across + 1) * piece,
                    ]
            for step in range(1, chips):
                send(part.at[lax.rem(chip + step, chips)], got.at[step], chip_peer(step), phase)

        def share_pieces(phase, share_phase, part, got, buffer):
            settle(recv_sem.at[stream, phase], got.at[pl.ds(1, chips - 1)])
            result = part[chip]
            for place in range(1, chips):
                result = result + got[place]
            buffer[chip] = result
            for step in range(1, chips):
                send(buffer.at[chip], buffer.at[chip], chip_peer(step), share_phase)

        def whole_pieces(buffer):
            return jnp.concatenate(
                [
                    jnp.concatenate([buffer[across * row_tiles + down] for down in range(row_tiles)], 0)
                    for across in range(chips // row_tiles)
                ],
                1,
            )

        def shared_pieces(phase, buffer):
            settle(recv_sem.at[stream, phase], buffer.at[pl.ds(1, chips - 1)])
            return whole_pieces(buffer)

        def half_product(buffer, stacked, side):
            return product_turned(whole(buffer, side), stacked[side])

        def gathered_product(phase, buffer, stacked):
            yield
            share_pair(phase, buffer)
            result = half_product(buffer, stacked, core)
            yield
            pair_arrived(phase, buffer)
            return result + half_product(buffer, stacked, other)

        live = live_blocks[0]
        if stream == 0:
            for place in range(4):
                loads[place].wait()
        updates = []
        contributions = []
        for k in range(blocks_here):
            residual = leaf_right[own_rows, k * width : (k + 1) * width]
            for child in range(k):
                residual = residual - jnp.where(parents[child] == k, updates[child], 0.0)
            block = jnp.where(k < live, product(residual, stack(leaf_inverse[k])), 0.0)
            solved[k] = block
            if k < blocks_here - 1:
                updates.append(product(block, stack(leaf_link[k])))
            contributions.append(product(block, stack(leaf_front[k])))
        spans = width // front_part
        for block in range(blocks_front):
            placed = jnp.zeros((columns, width), F32)
            for k in range(blocks_here):
                placed = placed + jnp.where(targets[k] == block, contributions[k], 0.0)
            for within in range(spans):
                owner = block * spans + within
                front_sum_part[owner % 2, owner // 2] = placed[
                    :, within * front_part : (within + 1) * front_part
                ]

        if stream == 0:
            pl.semaphore_wait(barrier, chips - 1 + quads - 1)
        send_pair(front_sum_part.at[other], front_sum_pair, FRONT_SUM)
        yield
        if stream == 0:
            loads[4].wait()
            loads[5].wait()
        pair_done(FRONT_SUM, front_sum_part, front_sum_pair)
        chip_send(FRONT_SUM, front_sum_part, front_sum_got)

        if stream == 0:
            split_rows(front_inverse, fi_stacked, front_part)
            for matrix in range(3):
                send_pair(half_of(matrix, other), root_halves.at[matrix, core], ROOT_SWAP)
        yield
        residual = front_right[own_rows, :] - total(FRONT_SUM, front_sum_part, front_sum_got)
        pair_sum(FRONT_SOLVE, front_solve_part, front_solve_pair, fill_blocks(residual, fi_stacked))
        yield
        pair_done(FRONT_SOLVE, front_solve_part, front_solve_pair)
        chip_send(FRONT_SOLVE, front_solve_part, front_solve_got)
        if stream == 0:
            loads[6].wait()
            level_part = level_rows // devs
            for level in range(2):
                split_rows(front_couple, fc_stacked.at[level], level_part, level * level_rows)
        yield
        front_forward = total(FRONT_SOLVE, front_solve_part, front_solve_got)

        pair_sum(
            RAISE_TOP, raise_top_part, raise_top_pair, fill_blocks(front_forward, fc_stacked.at[1])
        )
        yield
        pair_done(RAISE_TOP, raise_top_part, raise_top_pair)
        chip_send(RAISE_TOP, raise_top_part, raise_top_got)
        pair_sum(
            RAISE_LOW, raise_low_part, raise_low_pair, fill_blocks(front_forward, fc_stacked.at[0])
        )
        if stream == 0:
            for place in (7, 8, 9):
                loads[place].wait()
            settle(pair_recv_sem.at[stream, ROOT_SWAP], root_halves.at[:, 0])
            for matrix in range(3):
                split_root(matrix)
            turn(root_stacked.at[couple], root_turned.at[couple])
        yield
        pair_done(RAISE_LOW, raise_low_part, raise_low_pair)

        def less_right(level, values):
            return values - jnp.where(group == 0, root_right[own_rows, level, :], 0.0)

        yield
        raised_top = total(RAISE_TOP, raise_top_part, raise_top_got)
        share_quad(RAISE_TOP_QUAD, less_right(1, raised_top), raise_top_quad)
        chip_send(RAISE_LOW, raise_low_part, raise_low_got)

        yield
        residual = -pair_quad(RAISE_TOP_QUAD, raise_top_quad)
        send_pieces(TOP_SUM, product(residual, root_stacked[top_inverse]), top_part, top_got)
        if stream == 0:
            turn(root_stacked.at[low_inverse], root_turned.at[low_inverse])
            turn(root_stacked.at[top_inverse], root_turned.at[top_inverse])
        raised_low = total(RAISE_LOW, raise_low_part, raise_low_got)
        share_quad(RAISE_LOW_QUAD, less_right(0, raised_low), raise_low_quad)
        yield
        share_pieces(TOP_SUM, TOP_SHARE, top_part, top_got, top_share)
        low_right = -pair_quad(RAISE_LOW_QUAD, raise_low_quad)

        yield
        top_forward = shared_pieces(TOP_SHARE, top_share)
        share_quad(PUSH_QUAD, product_turned(top_forward, root_turned[couple]), push_quad)
        yield
        residual = low_right - total_quad(PUSH_QUAD, push_quad)
        send_pieces(LOW_SUM, product(residual, root_stacked[low_inverse]), low_part, low_got)
        if stream == 0:
            for side in range(2):
                turn(fc_stacked.at[0, side], fc_turned.at[0, side])
        yield
        share_pieces(LOW_SUM, LOW_SHARE, low_part, low_got, low_share)
        if stream == 0:
            for side in range(2):
                turn(fc_stacked.at[1, side], fc_turned.at[1, side])

        yield
        low_forward = shared_pieces(LOW_SHARE, low_share)
        back = product_turned(low_forward, root_turned[low_inverse])
        share_quad(LOW_BACK_QUAD, back, low_back_quad)
        yield
        low_pair = total_quad(LOW_BACK_QUAD, low_back_quad)
        send_pieces(CORRECT_SUM, product(low_pair, root_stacked[couple]), correct_part, correct_got)
        if stream == 0:
            for side in range(2):
                turn(fi_stacked.at[side], fi_turned.at[side])
        low_solution = own_side(low_pair)
        root_out[own_rows, 0, :] = low_solution
        yield
        share_pieces(CORRECT_SUM, CORRECT_SHARE, correct_part, correct_got, correct_share)
        share(LOW_ALL, low_solution, low_all)
        yield
        residual = whole_pieces(top_share) - shared_pieces(CORRECT_SHARE, correct_share)
        back = product_turned(residual, root_turned[top_inverse])
        share_quad(TOP_BACK_QUAD, back, top_back_quad)
        share_pair(LOW_ALL, low_all)
        yield
        top_solution = own_side(total_quad(TOP_BACK_QUAD, top_back_quad))
        share(TOP_ALL, top_solution, top_all)
        root_out[own_rows, 1, :] = top_solution
        lifted = half_product(low_all, fc_turned.at[0], core)
        pair_arrived(LOW_ALL, low_all)
        lifted = lifted + half_product(low_all, fc_turned.at[0], other)

        lifted = lifted + (yield from gathered_product(TOP_ALL, top_all, fc_turned.at[1]))
        share(REMAINDER_ALL, front_forward - lifted, remainder_all)
        front_values = yield from gathered_product(REMAINDER_ALL, remainder_all, fi_turned)
        share(FRONT_ALL, front_values, front_all)
        yield
        share_pair(FRONT_ALL, front_all)
        yield
        pair_arrived(FRONT_ALL, front_all)
        for owner in range(devs):
            front_out[own_rows, owner * front_part : (owner + 1) * front_part] = front_all[
                owner % 2, owner // 2
            ]

        solutions = [None] * blocks_here
        for k in reversed(range(blocks_here)):
            picked = jnp.zeros((columns, width), F32)
            for block in range(blocks_front):
                picked = picked + jnp.where(
                    targets[k] == block, front_out[own_rows, block * width : (block + 1) * width], 0.0
                )
            residual = solved[k] - product_transposed(picked, stack(leaf_front[k]))
            if k < blocks_here - 1:
                above = jnp.zeros((columns, width), F32)
                for upper in range(k + 1, blocks_here):
                    above = above + jnp.where(parents[k] == upper, solutions[upper], 0.0)
                residual = residual - product_transposed(above, stack(leaf_link[k]))
            solutions[k] = jnp.where(k < live, product_transposed(residual, stack(leaf_inverse[k])), 0.0)
            leaf_out[own_rows, k * width : (k + 1) * width] = solutions[k]

        yield
        for phase, buffer in (
            (FRONT_SUM, front_sum_part),
            (FRONT_SOLVE, front_solve_part),
            (RAISE_TOP, raise_top_part),
            (RAISE_LOW, raise_low_part),
            (LOW_ALL, low_all),
            (TOP_ALL, top_all),
            (REMAINDER_ALL, remainder_all),
            (FRONT_ALL, front_all),
        ):
            settle(send_sem.at[stream, phase], buffer.at[0, pl.ds(1, chips - 1)])
            settle(pair_send_sem.at[stream, phase], buffer.at[0])
        for phase, buffer in (
            (TOP_SUM, top_part),
            (TOP_SHARE, top_share),
            (LOW_SUM, low_part),
            (LOW_SHARE, low_share),
            (CORRECT_SUM, correct_part),
            (CORRECT_SHARE, correct_share),
        ):
            settle(send_sem.at[stream, phase], buffer.at[pl.ds(1, chips - 1)])
        for phase, buffer in (
            (RAISE_TOP_QUAD, raise_top_quad),
            (RAISE_LOW_QUAD, raise_low_quad),
            (PUSH_QUAD, push_quad),
            (LOW_BACK_QUAD, low_back_quad),
            (TOP_BACK_QUAD, top_back_quad),
        ):
            settle(send_sem.at[stream, phase], buffer.at[pl.ds(1, quads - 1)])
        if stream == 0:
            settle(pair_send_sem.at[stream, ROOT_SWAP], root_halves.at[:, 0])

    waiting = [solve(stream) for stream in range(STREAMS)]
    while waiting:
        waiting = [steps for steps in waiting if next(steps, True) is None]


def body(
    groups,
    devs,
    leaf_right,
    leaf_inverse,
    leaf_link,
    leaf_front,
    parents,
    front_rows,
    live_blocks,
    front_right,
    front_inverse,
    front_couple,
    root_right,
    root_inverse,
    root_couple,
):
    columns = leaf_right.shape[0]
    front_part = front_right.shape[1]
    level_part = root_right.shape[2]
    level_columns = root_inverse.shape[2]
    row_tiles = columns // STREAMS // ROW_TILE
    piece = level_columns // 2 * row_tiles // (devs // 2)
    own = columns // STREAMS
    loaded = (
        leaf_right,
        leaf_inverse,
        leaf_link,
        leaf_front,
        front_right,
        front_inverse,
        front_couple,
        root_inverse,
        root_couple,
    )
    rows, half = front_inverse.shape[0], front_inverse.shape[1] // 2
    level_half = front_couple.shape[1] // 4
    root_rows, root_half = root_inverse.shape[1], level_columns // 2
    halves = (
        (2, 2 * rows, half),
        (2, 2, 2 * rows, level_half),
        (3, 4 * root_rows, root_half),
    )
    chips = devs // 2
    front_full = pltpu.VMEM((STREAMS, 2, chips, own, front_part), F32)
    front_half = pltpu.VMEM((STREAMS, chips, own, front_part), F32)
    level_full = pltpu.VMEM((STREAMS, 2, chips, own, level_part), F32)
    level_half_blocks = pltpu.VMEM((STREAMS, chips, own, level_part), F32)
    pieces_half = pltpu.VMEM((STREAMS, chips, ROW_TILE, piece), F32)
    quad_blocks = pltpu.VMEM((STREAMS, 2 * groups, own, level_part), F32)
    quad_pairs = pltpu.VMEM((STREAMS, 2 * groups, own, 2 * level_part), F32)
    vmem = pl.BlockSpec(memory_space=pltpu.VMEM)
    smem = pl.BlockSpec(memory_space=pltpu.SMEM)
    anywhere = pl.BlockSpec(memory_space=pltpu.HBM)
    results = (
        jax.ShapeDtypeStruct(leaf_right.shape, F32),
        jax.ShapeDtypeStruct((columns, front_part * devs), F32),
        jax.ShapeDtypeStruct(root_right.shape, F32),
    )
    return pl.pallas_call(
        functools.partial(kernel, groups, devs),
        out_shape=results,
        in_specs=[smem] * 3 + [vmem] + [anywhere] * len(loaded),
        out_specs=(vmem, vmem, vmem),
        scratch_shapes=[pltpu.VMEM(array.shape, F32) for array in loaded[:-2]]
        + [pltpu.VMEM((3, 2, root_rows, root_half), F32)]
        + [pltpu.VMEM(shape, BF16) for shape in halves]
        + [pltpu.VMEM(shape[:-2] + (shape[-1], shape[-2]), BF16) for shape in halves]
        + [pltpu.VMEM((STREAMS, leaf_inverse.shape[0], own, leaf_inverse.shape[1]), F32)]
        + [front_full] * 2
        + [front_half] * 4
        + [level_full] * 2
        + [level_half_blocks] * 4
        + [pieces_half] * 9
        + [quad_blocks] * 2
        + [quad_pairs] * 3
        + [level_full] * 2
        + [front_full] * 2
        + [
            pltpu.SemaphoreType.DMA((len(loaded) + 1,)),
        ]
        + [pltpu.SemaphoreType.DMA((STREAMS, PHASES))] * 4,
        compiler_params=pltpu.CompilerParams(
            collective_id=0, has_side_effects=True, vmem_limit_bytes=60 * 1024 * 1024
        ),
        name="block_solves",
    )(parents, front_rows, live_blocks, root_right, *loaded)


def solution(mesh):
    in_specs = (
        P(None, ("grp", "dev")),
        P(("grp", "dev"), None, None),
        P(("grp", "dev"), None, None),
        P(("grp", "dev"), None, None),
        P(("grp", "dev")),
        P(("grp", "dev")),
        P(("grp", "dev")),
        P(None, ("grp", "dev")),
        P(("grp", "dev"), None),
        P(("grp", "dev"), None),
        P(None, None, "dev"),
        P(None, "dev", "grp"),
        P(None, "dev", "grp"),
    )
    out_specs = (P(None, ("grp", "dev")), P(None, "grp"), P(None, None, "dev"))
    return jax.shard_map(
        functools.partial(body, mesh.shape["grp"], mesh.shape["dev"]),
        mesh=mesh,
        in_specs=in_specs,
        out_specs=out_specs,
        check_vma=False,
    )
```
